32 devices in a mesh: shot: 4 (over y, x), mp: 8 (over z, core).
Axes of the slice: x: 2, y: 2, z: 4, core: 2. Of those that a mesh axis runs over, the one named last changes fastest.
Arguments:
- courant: float32 [2, 128, 64, 256], P(None, 'mp'), may hold values from 0.05 to 0.2
- aperture_first: int32 [4], P('shot'), may hold values from 0 to 8
- source_pos: int32 [4, 3], P('shot'), may hold values from 0 to 255, as said below
- wavelet: float32 [4, 4], P('shot'), may hold values from -6 to 6
- receiver_pos: int32 [4, 32, 3], P('shot'), may hold values from 0 to 255, as said below
- residual: float32 [4, 4, 32], P('shot'), may hold values from -6 to 6
- step_count: int32 [4], P('shot'), may hold values from 2 to 4
- forward_prev: float32 [4, 128, 64, 256], P('shot', 'mp'), may hold values from -1 to 1
- forward_now: float32 [4, 128, 64, 256], P('shot', 'mp'), may hold values from -1 to 1
- adjoint_prev: float32 [4, 128, 64, 256], P('shot', 'mp'), may hold values from -1 to 1
- adjoint_now: float32 [4, 128, 64, 256], P('shot', 'mp'), may hold values from -1 to 1
Outputs:
- gradient: float32 [2, 128, 64, 256], P(None, 'mp', 'shot')
The draws below stay inside these ranges and needn't reach their ends.
Inputs may be any that keep to these rules, and one draw needn't show every extreme that they name: `source_pos`: each component lies inside the aperture grid: first in 0..127, second in 0..63, third in 0..255. `receiver_pos`: each component lies inside the aperture grid (first in 0..127, second in 0..63, third in 0..255), within 12 cells of the shot's source along every dimension. The aperture covers model tiles aperture_first .. aperture_first + 7.
All inputs are finite; a program needn't handle non-finite values.
Results may differ from the reference program's by a relative error of at most 0.0003.
Values sent between devices are 32-bit elements; how exact they have to be, the bound alone decides.
A program may use at most 128 MiB of HBM per device.

```python
import math
import jax
import jax.numpy as jnp
from jax import lax

TX = 16
NY = 64
NZ = 256
SHOT_DEV = 1
RECV = 32
NT = 4
HALF = 128
SHOTS = 4
N_SHOT = 4
N_MP = 8


CIRCLE = 6.283185307179586


def corner_shot(key):
    return jax.random.randint(jax.random.fold_in(key, 5), (), 0, SHOTS)


def source_layout(key):
    first = jax.random.randint(jax.random.fold_in(key, 1), (SHOTS, 1), 0, HALF)
    second = jax.random.randint(jax.random.fold_in(key, 2), (SHOTS, 1), 0, NY)
    third = jax.random.randint(jax.random.fold_in(key, 3), (SHOTS, 1), 0, NZ)
    layout = jnp.concatenate([first, second, third], axis=1).astype(jnp.int32)
    corner = jnp.array([HALF - 1, NY - 1, NZ - 1], jnp.int32)
    return layout.at[corner_shot(key)].set(corner).astype(jnp.int32)


def draw_source_pos(key, part):
    return source_layout(jax.random.fold_in(key, 11))


def draw_receiver_pos(key, part):
    base = jax.random.fold_in(key, 11)
    source = source_layout(base)
    offsets = jax.random.randint(jax.random.fold_in(key, 23), (SHOTS, RECV, 3), -12, 13)
    offsets = offsets.at[corner_shot(base), 0].set(jnp.array([12, 12, 12], jnp.int32))
    limits = jnp.array([HALF - 1, NY - 1, NZ - 1], jnp.int32)
    placed = jnp.clip(source[:, None, :] + offsets, 0, limits[None, None, :])
    return placed.astype(jnp.int32)


def draw_step_count(key, part):
    counts = jax.random.randint(jax.random.fold_in(key, 31), (SHOTS,), NT // 2, NT + 1)
    chosen = jax.random.randint(jax.random.fold_in(key, 37), (), 0, SHOTS)
    return counts.at[chosen].set(NT).astype(jnp.int32)


def state_field(key, salt):
    base_key = jax.random.fold_in(key, salt)
    x_frac = (jnp.arange(HALF, dtype=jnp.float32)[None, :, None, None] + 0.5) / HALF
    y_frac = jnp.arange(NY, dtype=jnp.float32)[None, None, :, None] / NY
    z_frac = jnp.arange(NZ, dtype=jnp.float32)[None, None, None, :] / NZ
    freq = jax.random.randint(jax.random.fold_in(base_key, 2), (SHOTS, 3), 1, 4).astype(jnp.float32)
    phase = jax.random.uniform(jax.random.fold_in(base_key, 3), (SHOTS, 3), jnp.float32, -3.14159, 3.14159)
    wave_x = jnp.cos(CIRCLE * freq[:, 0][:, None, None, None] * x_frac + phase[:, 0][:, None, None, None])
    wave_y = jnp.cos(CIRCLE * freq[:, 1][:, None, None, None] * y_frac + phase[:, 1][:, None, None, None])
    wave_z = jnp.cos(CIRCLE * freq[:, 2][:, None, None, None] * z_frac + phase[:, 2][:, None, None, None])
    smooth = 0.08 * wave_x * wave_y * wave_z
    rough = 0.08 * jnp.clip(jax.random.normal(jax.random.fold_in(base_key, 1), (SHOTS, HALF, NY, NZ), jnp.float32), -5.0, 5.0)
    return (rough + smooth).astype(jnp.float32)


def draw_forward_prev(key, part):
    return state_field(key, 101)


def draw_forward_now(key, part):
    return state_field(key, 103)


def draw_adjoint_prev(key, part):
    return state_field(key, 107)


def draw_adjoint_now(key, part):
    return state_field(key, 109)


def with_ends(drawn, rng, least, high):
    place = [jax.random.randint(jax.random.fold_in(rng, axis), (), 0, length) for axis, length in enumerate(drawn.shape)]
    longest = drawn.shape.index(max(drawn.shape))
    next_to = place[:longest] + [(place[longest] + 1) % drawn.shape[longest]] + place[longest + 1:]
    return drawn.at[tuple(place)].set(least).at[tuple(next_to)].set(high)


def level_of(key, dims, split, low, high):
    gain = 1.0
    for dim, parts in split:
        heights = jax.random.uniform(jax.random.fold_in(jax.random.fold_in(key, 6), dim), (parts,), jnp.float32, low / len(split), high / len(split))
        gain = gain * jnp.repeat(jnp.exp(heights), dims[dim] // parts).reshape((-1,) + (1,) * (len(dims) - 1 - dim))
    return gain


def gaussian(stream_key, extent, deviation, bound, shards=(), kind=jnp.bfloat16):
    factor_of = level_of(stream_key, extent, shards, -0.22, 0.18) if shards else 1.0
    values = jax.random.normal(stream_key, extent, jnp.float32) * deviation * factor_of
    return jnp.minimum(jnp.maximum(values, -bound), bound).astype(kind)


def setup_inputs(seed: int = 0) -> dict:
    key_of = jax.random.split(jax.random.key(seed), 12)
    courant = jnp.clip(jnp.exp(math.log(0.2) - 1.3862944 * jax.random.uniform(key_of[0], (2, HALF, NY, NZ), jnp.float32) ** level_of(key_of[0], (2, HALF, NY, NZ), ((1, 8),), -0.2, 0.2)), 0.05, 0.2)
    aperture_first = with_ends(jax.random.randint(key_of[1], (N_SHOT,), 0, N_MP + 1), jax.random.fold_in(key_of[1], 1), 0, N_MP).astype(jnp.int32)
    source_pos = draw_source_pos(jax.random.fold_in(key_of[11], 71), 0)
    wavelet = gaussian(key_of[3], (SHOTS, NT), 1.0, 6.0, ((0, 4),), jnp.float32)
    receiver_pos = draw_receiver_pos(jax.random.fold_in(key_of[11], 71), 0)
    residual = gaussian(key_of[5], (SHOTS, NT, RECV), 1.0, 6.0, ((0, 4),), jnp.float32)
    step_count = draw_step_count(jax.random.fold_in(key_of[11], 71), 0)
    forward_prev = draw_forward_prev(jax.random.fold_in(key_of[11], 71), 0)
    forward_now = draw_forward_now(jax.random.fold_in(key_of[11], 71), 0)
    adjoint_prev = draw_adjoint_prev(jax.random.fold_in(key_of[11], 71), 0)
    adjoint_now = draw_adjoint_now(jax.random.fold_in(key_of[11], 71), 0)
    return dict(courant=courant, aperture_first=aperture_first, source_pos=source_pos, wavelet=wavelet, receiver_pos=receiver_pos, residual=residual, step_count=step_count, forward_prev=forward_prev, forward_now=forward_now, adjoint_prev=adjoint_prev, adjoint_now=adjoint_now)


COEF = (-205.0 / 72.0, 1.6, -0.2, 8.0 / 315.0, -1.0 / 560.0)


def laplace(field):
    xs, ys, zs = field.shape
    padded = jnp.pad(field, 4)
    total = 3.0 * COEF[0] * field
    for k in range(1, 5):
        total = total + COEF[k] * (padded[4 + k:4 + k + xs, 4:4 + ys, 4:4 + zs] + padded[4 - k:4 - k + xs, 4:4 + ys, 4:4 + zs])
        total = total + COEF[k] * (padded[4:4 + xs, 4 + k:4 + k + ys, 4:4 + zs] + padded[4:4 + xs, 4 - k:4 - k + ys, 4:4 + zs])
        total = total + COEF[k] * (padded[4:4 + xs, 4:4 + ys, 4 + k:4 + k + zs] + padded[4:4 + xs, 4:4 + ys, 4 - k:4 - k + zs])
    return total


def reference(courant, aperture_first, source_pos, wavelet, receiver_pos, residual, step_count, forward_prev, forward_now, adjoint_prev, adjoint_now):
    model = courant.reshape(2 * HALF, NY, NZ)
    zeros = jnp.zeros((HALF, NY, NZ), jnp.float32)

    def one_shot(grad, shot_index):
        group = shot_index // SHOT_DEV
        start = (aperture_first[group] * TX).astype(jnp.int32)
        speed = lax.dynamic_slice_in_dim(model, start, HALF, 0)
        source = source_pos[shot_index]
        receivers = receiver_pos[shot_index]
        count = step_count[shot_index]
        u_prev, u_now = forward_prev[shot_index], forward_now[shot_index]
        stored = []
        for n in range(NT):
            force = zeros.at[source[0], source[1], source[2]].add(wavelet[shot_index, n])
            drive = laplace(u_now) + force
            u_next = 2.0 * u_now - u_prev + speed * drive
            active = n < count
            stored.append(jnp.where(active, drive, 0.0))
            u_prev, u_now = jnp.where(active, u_now, u_prev), jnp.where(active, u_next, u_now)
        w_prev, w_now = adjoint_prev[shot_index], adjoint_now[shot_index]
        image = zeros
        for k in range(NT):
            n = NT - 1 - k
            inject = zeros.at[receivers[:, 0], receivers[:, 1], receivers[:, 2]].add(residual[shot_index, n])
            w_next = 2.0 * w_now - w_prev + speed * (laplace(w_now) + inject)
            active = n < count
            image = image + jnp.where(active, w_next * stored[n], 0.0)
            w_prev, w_now = jnp.where(active, w_now, w_prev), jnp.where(active, w_next, w_now)
        window = lax.dynamic_slice_in_dim(grad, start, HALF, 0)
        grad = lax.dynamic_update_slice_in_dim(grad, window + image, start, 0)
        return grad, None

    grad, unused = lax.scan(one_shot, jnp.zeros((2 * HALF, NY, NZ), jnp.float32), jnp.arange(SHOTS, dtype=jnp.int32))
    return grad.reshape(2, HALF, NY, NZ)
```

```python
import functools

import jax
import jax.numpy as jnp
from jax import lax
from jax.experimental import pallas as pl
from jax.experimental.pallas import tpu as pltpu
from jax.sharding import PartitionSpec as P

COEF = (-205.0 / 72.0, 1.6, -0.2, 8.0 / 315.0, -1.0 / 560.0)
F32 = jnp.float32
BF16 = jnp.bfloat16
MESH = pl.DeviceIdType.MESH
CHUNK = 4
STEPS = 4


def band(size, centre):
    row = lax.broadcasted_iota(jnp.int32, (size, size), 0)
    col = lax.broadcasted_iota(jnp.int32, (size, size), 1)
    gap = jnp.abs(row - col)
    value = jnp.where(gap == 0, centre, 0.0)
    for k in range(1, 5):
        value = jnp.where(gap == k, COEF[k], value)
    high = value.astype(BF16)
    return high, (value - high.astype(F32)).astype(BF16)


def kernel(
    n, groups, tx, ny, nz, recv,
    first_ref, source_ref, wave_ref, count_ref, rec_ref, rect_ref, res_ref,
    courant, fprev, fnow, aprev, anow,
    out_ref,
    u_buf, w_buf, u_old, w_old, e_buf, d_buf, inj, p_buf,
    tiles, staged, landed, img, shared, pieces, acc, firsts, zmat, ymat, smask, rmat,
    load_sem, halo_send, halo_recv, f_send, f_recv, a_send, a_recv, b_send, b_recv,
    x_send, x_recv, i_send, i_recv, g_send, g_recv, o_send, o_recv,
):
    me = lax.axis_index("mp")
    mine = lax.axis_index("shot")
    q = ny // groups
    gx = min(n, tx)
    gz = n // gx
    px, pz = tx // gx, nz // gz
    chunks = tx // CHUNK
    per = n // chunks
    myc = lax.div(me, per)

    def spot(k):
        if gz == 1:
            return pl.ds(k * px, px), pl.ds(0, nz)
        return (
            pl.ds(lax.div(k, gz) * px, px),
            pl.ds(pl.multiple_of(lax.rem(k, gz) * pz, pz), pz),
        )

    def strip(s):
        return pl.ds(pl.multiple_of(s * q, q), q)

    def others(count, own, visit):
        def go(o, carry):
            visit(lax.rem(own + o, count))
            return carry

        lax.fori_loop(1, count, go, 0)

    def loop(count, visit):
        def go(o, carry):
            visit(o)
            return carry

        lax.fori_loop(0, count, go, 0)

    def remote(src, dst, send, recv_, target):
        return pltpu.make_async_remote_copy(
            src_ref=src, dst_ref=dst, send_sem=send, recv_sem=recv_,
            device_id=target, device_id_type=MESH,
        )

    barrier = pltpu.get_barrier_semaphore()
    others(n, me, lambda k: pl.semaphore_signal(
        barrier, inc=1, device_id={"mp": k}, device_id_type=MESH))
    others(groups, mine, lambda s: pl.semaphore_signal(
        barrier, inc=1, device_id={"shot": s}, device_id_type=MESH))
    pl.semaphore_wait(barrier, n - 1 + groups - 1)

    def model_copy(k, sender):
        xs, zs = spot(k)
        return remote(
            courant.at[:, xs, strip(mine), zs], tiles.at[:, sender],
            a_send.at[k], a_recv.at[sender], {"mp": k})

    def first_copy(s, sender):
        return remote(firsts.at[sender], firsts.at[sender], f_send.at[s], f_recv.at[sender], {"shot": s})

    firsts[pl.ds(mine, 1)] = jnp.full((1, 8, 128), first_ref[0], jnp.int32)
    others(groups, mine, lambda s: first_copy(s, mine).start())
    others(n, me, lambda k: model_copy(k, me).start())
    my_x, my_z = spot(me)
    own_tile = pltpu.make_async_copy(
        courant.at[:, my_x, strip(mine), my_z], tiles.at[:, me], load_sem.at[4])
    own_tile.start()

    def halo(f, t, side, src):
        buf = (u_buf, w_buf)[f]
        dst = buf.at[t, pl.ds(0, 4)] if side == 0 else buf.at[t, pl.ds(tx + 4, 4)]
        target = me + 1 if side == 0 else me - 1
        return remote(src, dst, halo_send.at[f, t, side], halo_recv.at[f, t, side], {"mp": target})

    def halo_src(f, t, side):
        if t == 0:
            src = (fnow, anow)[f]
            return src.at[0, pl.ds(tx - 4, 4)] if side == 0 else src.at[0, pl.ds(0, 4)]
        buf = (u_buf, w_buf)[f]
        return buf.at[t, pl.ds(tx, 4)] if side == 0 else buf.at[t, pl.ds(4, 4)]

    def send_halo(f, t):
        @pl.when(me < n - 1)
        def _():
            halo(f, t, 0, halo_src(f, t, 0)).start()

        @pl.when(me > 0)
        def _():
            halo(f, t, 1, halo_src(f, t, 1)).start()

    def wait_halo(f, t):
        @pl.when(me > 0)
        def _():
            halo(f, t, 0, halo_src(f, t, 0)).wait_recv()

        @pl.when(me < n - 1)
        def _():
            halo(f, t, 1, halo_src(f, t, 1)).wait_recv()

    def drain_halo(f, t):
        @pl.when(me < n - 1)
        def _():
            halo(f, t, 0, halo_src(f, t, 0)).wait_send()

        @pl.when(me > 0)
        def _():
            halo(f, t, 1, halo_src(f, t, 1)).wait_send()

    send_halo(0, 0)
    send_halo(1, 0)
    loads = [
        pltpu.make_async_copy(fnow.at[0], u_buf.at[0, pl.ds(4, tx)], load_sem.at[0]),
        pltpu.make_async_copy(anow.at[0], w_buf.at[0, pl.ds(4, tx)], load_sem.at[1]),
        pltpu.make_async_copy(fprev.at[0], u_old, load_sem.at[2]),
        pltpu.make_async_copy(aprev.at[0], w_old, load_sem.at[3]),
    ]
    for copy in loads:
        copy.start()

    edge = jnp.zeros((4, ny, nz), F32)

    @pl.when(me == 0)
    def _():
        for t in range(STEPS):
            u_buf[t, pl.ds(0, 4)] = edge
            w_buf[t, pl.ds(0, 4)] = edge

    @pl.when(me == n - 1)
    def _():
        for t in range(STEPS):
            u_buf[t, pl.ds(tx + 4, 4)] = edge
            w_buf[t, pl.ds(tx + 4, 4)] = edge

    high, low = band(nz, 3.0 * COEF[0])
    zmat[pl.ds(0, nz)] = high
    zmat[pl.ds(nz, nz)] = high
    zmat[pl.ds(2 * nz, nz)] = low
    high, low = band(ny, 0.0)
    ymat[...] = jnp.concatenate([high, high, low], axis=1)
    y_id = lax.broadcasted_iota(jnp.int32, (ny, nz), 0)
    z_id = lax.broadcasted_iota(jnp.int32, (ny, nz), 1)
    smask[...] = jnp.where((y_id == source_ref[0, 1]) & (z_id == source_ref[0, 2]), 1.0, 0.0)
    hit_z = rec_ref[:, 2:3] == lax.broadcasted_iota(jnp.int32, (recv, nz), 1)
    hit_z = jnp.where(hit_z, 1.0, 0.0).astype(BF16)
    for i in range(3):
        rmat[pl.ds(i * recv, recv)] = hit_z
    res = res_ref[...]
    res0 = res.astype(BF16).astype(F32)
    res1 = (res - res0).astype(BF16).astype(F32)
    res2 = res - res0 - res1
    res_all = jnp.concatenate([res0, res1, res2], axis=1)
    rec_all = jnp.concatenate([rect_ref[...]] * 3, axis=1)
    hit_y = lax.broadcasted_iota(jnp.int32, (ny, 3 * recv), 0) == rec_all[1:2]
    hit_y = jnp.where(hit_y, 1.0, 0.0)

    def inject(c):
        x0 = c * CHUNK
        for s in range(STEPS):
            rows = []
            for i in range(CHUNK):
                at_x = jnp.where(rec_all[0:1] == me * tx + x0 + i, res_all[s:s + 1], 0.0)
                rows.append((hit_y * at_x).astype(BF16))
            field = jnp.dot(jnp.concatenate(rows, axis=0), rmat[...], preferred_element_type=F32)
            inj[s, pl.ds(x0, CHUNK)] = field.reshape(CHUNK, ny, nz)

    loop(chunks, inject)

    own_tile.wait()
    others(n, me, lambda k: model_copy(k, k).wait_recv())
    others(groups, mine, lambda s: first_copy(s, s).wait_recv())
    starts = [jnp.max(firsts[s]) for s in range(groups)]

    def pick(m):
        for s in range(groups):
            t = m + starts[s]
            staged[m, s] = tiles[lax.div(t, n), lax.rem(t, n)]

    def spread_copy(m, sender):
        xs, zs = spot(sender)
        return remote(
            staged.at[m], landed.at[:, xs, :, zs],
            b_send.at[m], b_recv.at[sender], {"mp": m})

    def pick_send(m):
        pick(m)
        spread_copy(m, me).start()

    others(n, me, pick_send)
    pick(me)
    keep_own = pltpu.make_async_copy(staged.at[me], landed.at[:, my_x, :, my_z], load_sem.at[5])
    keep_own.start()

    def lap(buf, t, x0):
        centre = buf[t, pl.ds(x0 + 4, CHUNK)].reshape(CHUNK * ny, nz)
        high = centre.astype(BF16)
        low = (centre - high.astype(F32)).astype(BF16)
        along_z = jnp.dot(
            jnp.concatenate([high, low, high], axis=1), zmat[...], preferred_element_type=F32)
        along_y = []
        for i in range(CHUNK):
            rows = slice(i * ny, (i + 1) * ny)
            stack = jnp.concatenate([high[rows], low[rows], high[rows]], axis=0)
            along_y.append(jnp.dot(ymat[...], stack, preferred_element_type=F32))
        total = along_z.reshape(CHUNK, ny, nz) + jnp.stack(along_y)
        for k in range(1, 5):
            total = total + COEF[k] * (
                buf[t, pl.ds(x0 + 4 + k, CHUNK)] + buf[t, pl.ds(x0 + 4 - k, CHUNK)])
        return total

    count = count_ref[0]
    source_x = source_ref[0, 0] - me * tx

    def drive(t, x0):
        total = lap(u_buf, t, x0)
        parts = []
        for i in range(CHUNK):
            amount = jnp.where(source_x == x0 + i, wave_ref[0, t], 0.0)
            parts.append(total[i] + smask[...] * amount)
        total = jnp.stack(parts)
        if t >= 2:
            total = jnp.where(t < count, total, 0.0)
        return total

    def forward(t, x0):
        own = pl.ds(x0, CHUNK)
        mid = pl.ds(x0 + 4, CHUNK)
        if t == 0:
            total, before = d_buf[0, own], u_old[own]
        else:
            total = drive(t, x0)
            d_buf[t, own] = total
            before = u_old[own] if t == 0 else u_buf[t - 1, mid]
        u_buf[t + 1, mid] = 2.0 * u_buf[t, mid] - before + p_buf[own] * total

    def backward(t, x0):
        own = pl.ds(x0, CHUNK)
        mid = pl.ds(x0 + 4, CHUNK)
        s = STEPS - 1 - t
        total = e_buf[own] if t == 0 else lap(w_buf, t, x0) + inj[s, own]
        now = w_buf[t, mid]
        before = w_buf[t - 1, mid] if s + 1 < 2 else w_old[own]
        new = 2.0 * now - before + p_buf[own] * total
        if s >= 2:
            w_old[own] = jnp.where(s < count, now, before)
            new = jnp.where(s < count, new, now)
        return new

    def adjoint(t, x0):
        w_buf[t + 1, pl.ds(x0 + 4, CHUNK)] = backward(t, x0)

    last = tx - CHUNK
    faces = lambda visit: loop(2, lambda i: visit(i * last))
    inner = lambda visit: loop(chunks - 2, lambda i: visit(CHUNK + i * CHUNK))

    for copy in loads:
        copy.wait()

    def early(x0):
        d_buf[0, pl.ds(x0, CHUNK)] = drive(0, x0)
        e_buf[pl.ds(x0, CHUNK)] = lap(w_buf, 0, x0) + inj[STEPS - 1, pl.ds(x0, CHUNK)]

    inner(early)
    wait_halo(0, 0)
    wait_halo(1, 0)
    faces(early)

    def hand_copy(c, s, sender):
        xs = pl.ds(c * CHUNK, CHUNK)
        return remote(
            landed.at[s, xs], p_buf.at[xs, strip(sender)],
            x_send.at[c, s], x_recv.at[c, sender], {"shot": s})

    keep_own.wait()

    def hand(i):
        c = lax.rem(myc - i + chunks, chunks)

        def arrive(j):
            k = c * per + j

            @pl.when(k != me)
            def _():
                spread_copy(k, k).wait_recv()

        loop(per, arrive)
        others(groups, mine, lambda s: hand_copy(c, s, mine).start())
        xs = pl.ds(c * CHUNK, CHUNK)
        p_buf[xs, strip(mine)] = landed[pl.ds(mine, 1), xs].reshape(CHUNK, q, nz)

    loop(chunks, hand)

    def handed(c):
        others(groups, mine, lambda s: hand_copy(c, s, s).wait_recv())

    loop(chunks, handed)

    for t in range(STEPS - 1):
        if t:
            wait_halo(0, t)
        faces(functools.partial(forward, t))
        send_halo(0, t + 1)
        inner(functools.partial(forward, t))
        if t:
            wait_halo(1, t)
        faces(functools.partial(adjoint, t))
        send_halo(1, t + 1)
        inner(functools.partial(adjoint, t))

    def image_copy(c, s, sender):
        xs = pl.ds(c * CHUNK, CHUNK)
        return remote(
            img.at[xs, strip(s)], shared.at[sender, xs],
            i_send.at[c, s], i_recv.at[c, sender], {"shot": s})

    def final(x0):
        own = pl.ds(x0, CHUNK)
        mid = pl.ds(x0 + 4, CHUNK)
        t = STEPS - 1
        new = backward(t, x0) * d_buf[0, own]
        new = new + w_buf[1, mid] * drive(t, x0)
        for k in range(1, t):
            new = new + w_buf[k + 1, mid] * d_buf[t - k, own]
        img[own] = new
        c = lax.div(x0, CHUNK)
        others(groups, mine, lambda s: image_copy(c, s, mine).start())
        shared[pl.ds(mine, 1), own] = img[own, strip(mine)].reshape(1, CHUNK, q, nz)

    inner(final)
    wait_halo(0, STEPS - 1)
    wait_halo(1, STEPS - 1)
    faces(final)

    def piece_copy(k, sender):
        xs, zs = spot(k)
        return remote(
            shared.at[:, xs, :, zs], pieces.at[sender],
            g_send.at[k], g_recv.at[sender], {"mp": k})

    def scatter(x0):
        c = lax.div(x0, CHUNK)
        others(groups, mine, lambda s: image_copy(c, s, s).wait_recv())

        def go(j):
            k = c * per + j

            @pl.when(k != me)
            def _():
                piece_copy(k, me).start()

        loop(per, go)

    inner(scatter)
    faces(scatter)
    keep_piece = pltpu.make_async_copy(shared.at[:, my_x, :, my_z], pieces.at[me], load_sem.at[6])
    keep_piece.start()
    keep_piece.wait()
    others(n, me, lambda k: piece_copy(k, k).wait_recv())

    def out_copy(i, sender):
        xs, zs = spot(sender)
        return remote(
            acc.at[i], out_ref.at[:, xs, :, zs], o_send.at[i], o_recv.at[sender], {"mp": i})

    def total(i):
        for r in range(2):
            value = jnp.zeros((px, q, pz), F32)
            for s in range(groups):
                m = i + r * n - starts[s]
                inside = (m >= 0) & (m < n)
                piece = pieces[jnp.clip(m, 0, n - 1), s]
                value = value + jnp.where(inside, piece, 0.0)
            acc[i, r] = value

    def total_send(i):
        total(i)
        out_copy(i, me).start()

    others(n, me, total_send)
    total(me)
    keep_out = pltpu.make_async_copy(acc.at[me], out_ref.at[:, my_x, :, my_z], load_sem.at[7])
    keep_out.start()
    keep_out.wait()
    others(n, me, lambda k: out_copy(k, k).wait_recv())

    others(groups, mine, lambda s: first_copy(s, mine).wait_send())
    others(n, me, lambda k: model_copy(k, me).wait_send())
    others(n, me, lambda k: spread_copy(k, me).wait_send())
    loop(chunks, lambda c: others(groups, mine, lambda s: hand_copy(c, s, mine).wait_send()))
    loop(chunks, lambda c: others(groups, mine, lambda s: image_copy(c, s, mine).wait_send()))
    others(n, me, lambda k: piece_copy(k, me).wait_send())
    others(n, me, lambda k: out_copy(k, me).wait_send())
    for t in range(STEPS):
        drain_halo(0, t)
        drain_halo(1, t)


def body(
    courant, aperture_first, source_pos, wavelet, receiver_pos, residual, step_count,
    forward_prev, forward_now, adjoint_prev, adjoint_now,
):
    n = lax.axis_size("mp")
    groups = lax.axis_size("shot")
    tx, ny, nz = courant.shape[1:]
    recv = receiver_pos.shape[1]
    q = ny // groups
    gx = min(n, tx)
    gz = n // gx
    px, pz = tx // gx, nz // gz
    chunks = tx // CHUNK
    smem = pl.BlockSpec(memory_space=pltpu.SMEM)
    vmem = pl.BlockSpec(memory_space=pltpu.VMEM)
    hbm = pl.BlockSpec(memory_space=pl.ANY)
    dma = pltpu.SemaphoreType.DMA
    return pl.pallas_call(
        functools.partial(kernel, n, groups, tx, ny, nz, recv),
        out_shape=jax.ShapeDtypeStruct((2, tx, q, nz), F32),
        in_specs=[smem] * 4 + [vmem] * 3 + [hbm] * 5,
        out_specs=vmem,
        scratch_shapes=[
            pltpu.VMEM((STEPS, tx + 8, ny, nz), F32),
            pltpu.VMEM((STEPS, tx + 8, ny, nz), F32),
            pltpu.VMEM((tx, ny, nz), F32),
            pltpu.VMEM((tx, ny, nz), F32),
            pltpu.VMEM((tx, ny, nz), F32),
            pltpu.VMEM((STEPS - 1, tx, ny, nz), F32),
            pltpu.VMEM((STEPS, tx, ny, nz), F32),
            pltpu.VMEM((tx, ny, nz), F32),
            pltpu.VMEM((2, n, px, q, pz), F32),
            pltpu.VMEM((n, groups, px, q, pz), F32),
            pltpu.VMEM((groups, tx, q, nz), F32),
            pltpu.VMEM((tx, ny, nz), F32),
            pltpu.VMEM((groups, tx, q, nz), F32),
            pltpu.VMEM((n, groups, px, q, pz), F32),
            pltpu.VMEM((n, 2, px, q, pz), F32),
            pltpu.VMEM((groups, 8, 128), jnp.int32),
            pltpu.VMEM((3 * nz, nz), BF16),
            pltpu.VMEM((ny, 3 * ny), BF16),
            pltpu.VMEM((ny, nz), F32),
            pltpu.VMEM((3 * recv, nz), BF16),
            dma((8,)),
            dma((2, STEPS, 2)), dma((2, STEPS, 2)),
            dma((groups,)), dma((groups,)),
            dma((n,)), dma((n,)),
            dma((n,)), dma((n,)),
            dma((chunks, groups)), dma((chunks, groups)),
            dma((chunks, groups)), dma((chunks, groups)),
            dma((n,)), dma((n,)),
            dma((n,)), dma((n,)),
        ],
        compiler_params=pltpu.CompilerParams(
            collective_id=0, has_side_effects=True, vmem_limit_bytes=58 * 1024 * 1024),
    )(
        aperture_first, source_pos, wavelet, step_count,
        receiver_pos[0], receiver_pos[0].T, residual[0],
        courant, forward_prev, forward_now, adjoint_prev, adjoint_now,
    )


def solution(mesh):
    return jax.shard_map(
        body,
        mesh=mesh,
        in_specs=(
            P(None, "mp", None, None),
            P("shot"),
            P("shot", None),
            P("shot", None),
            P("shot", None, None),
            P("shot", None, None),
            P("shot"),
            P("shot", "mp", None, None),
            P("shot", "mp", None, None),
            P("shot", "mp", None, None),
            P("shot", "mp", None, None),
        ),
        out_specs=P(None, "mp", "shot", None),
        check_vma=False,
    )
```

```python
import functools

import jax
import jax.numpy as jnp
from jax import lax
from jax.experimental import pallas as pl
from jax.experimental.pallas import tpu as pltpu
from jax.sharding import PartitionSpec as P

COEF = (-205.0 / 72.0, 1.6, -0.2, 8.0 / 315.0, -1.0 / 560.0)
F32 = jnp.float32
BF16 = jnp.bfloat16
MESH = pl.DeviceIdType.MESH
CHUNK = 4
STEPS = 4
HALVES = 2


def band(size, centre):
    row = lax.broadcasted_iota(jnp.int32, (size, size), 0)
    col = lax.broadcasted_iota(jnp.int32, (size, size), 1)
    gap = jnp.abs(row - col)
    value = jnp.where(gap == 0, centre, 0.0)
    for k in range(1, 5):
        value = jnp.where(gap == k, COEF[k], value)
    high = value.astype(BF16)
    return high, (value - high.astype(F32)).astype(BF16)


def kernel(
    n, groups, tx, ny, nz, recv,
    first_ref, source_ref, wave_ref, count_ref, rec_ref, res_ref,
    courant, fprev, fnow, aprev, anow,
    out_ref,
    u_buf, w_buf, u_old, w_old, e_buf, d_buf, inj, p_buf,
    tiles, staged, img, shared, beside, part, arrived, firsts, zmat, ymat, smask, rmat,
    load_sem, halo_send, halo_recv, f_send, f_recv, a_send, a_recv, b_send, b_recv,
    x_send, x_recv, i_send, i_recv, g_send, g_recv, o_send, o_recv,
):
    me = lax.axis_index("mp")
    mine = lax.axis_index("shot")
    chip, core = lax.div(me, 2), lax.rem(me, 2)
    sibling = me + 1 - 2 * core
    line = n // 2
    q = ny // groups
    chunks = tx // CHUNK
    half = tx // HALVES

    def strip(s):
        return pl.ds(pl.multiple_of(s * q, q), q)

    def others(count, own, visit):
        def go(o, carry):
            visit(lax.rem(own + o, count))
            return carry

        lax.fori_loop(1, count, go, 0)

    def loop(count, visit):
        def go(o, carry):
            visit(o)
            return carry

        lax.fori_loop(0, count, go, 0)

    def remote(src, dst, send, recv_, target):
        return pltpu.make_async_remote_copy(
            src_ref=src, dst_ref=dst, send_sem=send, recv_sem=recv_,
            device_id=target, device_id_type=MESH,
        )

    barrier = pltpu.get_barrier_semaphore()
    nearby = [(me - 1, me >= 1), (me + 1, me < n - 1), (me - 2, me >= 2), (me + 2, me < n - 2)]
    for k, there in nearby:
        @pl.when(there)
        def _(k=k):
            pl.semaphore_signal(barrier, inc=1, device_id={"mp": k}, device_id_type=MESH)
    others(groups, mine, lambda s: pl.semaphore_signal(
        barrier, inc=1, device_id={"shot": s}, device_id_type=MESH))
    peers = groups - 1 + jnp.minimum(me, 2) + jnp.minimum(n - 1 - me, 2)
    pl.semaphore_wait(barrier, peers)

    def tile_ref(h, r, z, c):
        return tiles.at[r, 2 * z + c, pl.ds(h * half, half)]

    def own_ref(h, r):
        return courant.at[r, pl.ds(h * half, half), strip(mine)]

    def along(h, r, z, src):
        return remote(
            src, tile_ref(h, r, z, core), a_send.at[h, r, z], a_recv.at[h, r, z],
            {"mp": me - 2 if r == 0 else me + 2})

    def across(h, r, z, src, c):
        return remote(
            src, tile_ref(h, r, z, c), b_send.at[h, r, z], b_recv.at[h, r, z], {"mp": sibling})

    def onward(r):
        return chip > 0 if r == 0 else chip < line - 1

    def send_own(h):
        for r in range(2):
            @pl.when(onward(r))
            def _():
                along(h, r, chip, own_ref(h, r)).start()
        for r in range(2):
            across(h, r, chip, own_ref(h, r), core).start()

    def hop(h, d):
        for r in range(2):
            z = chip + d if r == 0 else chip - d
            there = z < line if r == 0 else z >= 0

            @pl.when(there)
            def _():
                along(h, r, z, tile_ref(h, r, z, core)).wait_recv()

                @pl.when(onward(r))
                def _():
                    along(h, r, z, tile_ref(h, r, z, core)).start()

                across(h, r, z, tile_ref(h, r, z, core), core).start()

    def each_tile(visit):
        for d in range(line):
            for r in range(2):
                z = chip + d if r == 0 else chip - d

                @pl.when(z < line if r == 0 else z >= 0)
                def _():
                    visit(r, z)

    def first_copy(s, sender):
        return remote(firsts.at[sender], firsts.at[sender], f_send.at[s], f_recv.at[sender], {"shot": s})

    send_own(0)
    firsts[pl.ds(mine, 1)] = jnp.full((1, 8, 128), first_ref[0], jnp.int32)
    others(groups, mine, lambda s: first_copy(s, mine).start())
    own_tile = pltpu.make_async_copy(courant.at[:, :, strip(mine)], tiles.at[:, me], load_sem.at[4])
    own_tile.start()

    def halo(f, t, side, src):
        buf = (u_buf, w_buf)[f]
        dst = buf.at[t, pl.ds(0, 4)] if side == 0 else buf.at[t, pl.ds(tx + 4, 4)]
        target = me + 1 if side == 0 else me - 1
        return remote(src, dst, halo_send.at[f, t, side], halo_recv.at[f, t, side], {"mp": target})

    def halo_src(f, t, side):
        if t == 0:
            src = (fnow, anow)[f]
            return src.at[0, pl.ds(tx - 4, 4)] if side == 0 else src.at[0, pl.ds(0, 4)]
        buf = (u_buf, w_buf)[f]
        return buf.at[t, pl.ds(tx, 4)] if side == 0 else buf.at[t, pl.ds(4, 4)]

    def send_halo(f, t):
        @pl.when(me < n - 1)
        def _():
            halo(f, t, 0, halo_src(f, t, 0)).start()

        @pl.when(me > 0)
        def _():
            halo(f, t, 1, halo_src(f, t, 1)).start()

    def wait_halo(f, t):
        @pl.when(me > 0)
        def _():
            halo(f, t, 0, halo_src(f, t, 0)).wait_recv()

        @pl.when(me < n - 1)
        def _():
            halo(f, t, 1, halo_src(f, t, 1)).wait_recv()

    def drain_halo(f, t):
        @pl.when(me < n - 1)
        def _():
            halo(f, t, 0, halo_src(f, t, 0)).wait_send()

        @pl.when(me > 0)
        def _():
            halo(f, t, 1, halo_src(f, t, 1)).wait_send()

    loads = [
        pltpu.make_async_copy(fnow.at[0], u_buf.at[0, pl.ds(4, tx)], load_sem.at[0]),
        pltpu.make_async_copy(anow.at[0], w_buf.at[0, pl.ds(4, tx)], load_sem.at[1]),
        pltpu.make_async_copy(fprev.at[0], u_old, load_sem.at[2]),
        pltpu.make_async_copy(aprev.at[0], w_old, load_sem.at[3]),
    ]
    for copy in loads:
        copy.start()

    edge = jnp.zeros((4, ny, nz), F32)

    @pl.when(me == 0)
    def _():
        for t in range(STEPS):
            u_buf[t, pl.ds(0, 4)] = edge
            w_buf[t, pl.ds(0, 4)] = edge

    @pl.when(me == n - 1)
    def _():
        for t in range(STEPS):
            u_buf[t, pl.ds(tx + 4, 4)] = edge
            w_buf[t, pl.ds(tx + 4, 4)] = edge

    high, low = band(nz, 3.0 * COEF[0])
    zmat[pl.ds(0, nz)] = high
    zmat[pl.ds(nz, nz)] = high
    zmat[pl.ds(2 * nz, nz)] = low
    high, low = band(ny, 0.0)
    ymat[...] = jnp.concatenate([high, high, low], axis=1)
    y_id = lax.broadcasted_iota(jnp.int32, (ny, nz), 0)
    z_id = lax.broadcasted_iota(jnp.int32, (ny, nz), 1)
    smask[...] = jnp.where((y_id == source_ref[0, 1]) & (z_id == source_ref[0, 2]), 1.0, 0.0)
    same = (lax.broadcasted_iota(jnp.int32, (recv, recv), 0)
            == lax.broadcasted_iota(jnp.int32, (recv, recv), 1))
    at_z = jnp.sum(jnp.where(same, rec_ref[2].astype(F32), 0.0), axis=1, keepdims=True)
    hit_z = at_z.astype(jnp.int32) == lax.broadcasted_iota(jnp.int32, (recv, nz), 1)
    hit_z = jnp.where(hit_z, 1.0, 0.0).astype(BF16)
    for i in range(3):
        rmat[pl.ds(i * recv, recv)] = hit_z
    res = res_ref[0]
    res0 = res.astype(BF16).astype(F32)
    res1 = (res - res0).astype(BF16).astype(F32)
    res2 = res - res0 - res1
    res_all = jnp.concatenate([res0, res1, res2], axis=1)
    rec_x = jnp.concatenate([rec_ref[0]] * 3, axis=1)
    rec_y = jnp.concatenate([rec_ref[1]] * 3, axis=1)
    hit_y = lax.broadcasted_iota(jnp.int32, (ny, 3 * recv), 0) == rec_y
    hit_y = jnp.where(hit_y, 1.0, 0.0)

    def inject(c):
        x0 = c * CHUNK
        for s in range(STEPS):
            rows = []
            for i in range(CHUNK):
                at_x = jnp.where(rec_x == me * tx + x0 + i, res_all[s:s + 1], 0.0)
                rows.append((hit_y * at_x).astype(BF16))
            field = jnp.dot(jnp.concatenate(rows, axis=0), rmat[...], preferred_element_type=F32)
            inj[s, pl.ds(x0, CHUNK)] = field.reshape(CHUNK, ny, nz)

    def hand_copy(h, s, sender):
        xs = pl.ds(h * half, half)
        return remote(
            staged.at[s, xs], p_buf.at[xs, strip(sender)],
            x_send.at[h, s], x_recv.at[h, sender], {"shot": s})

    def picked(s, x):
        first = jnp.max(firsts[pl.ds(s, 1)])
        value = jnp.zeros((1, q, nz), F32)
        for k in range(n + 1):
            t = me + k
            value = jnp.where(first == k, tiles[lax.div(t, n), lax.rem(t, n), pl.ds(x, 1)], value)
        return value

    def hand(h):
        each_tile(lambda r, z: across(h, r, z, tile_ref(h, r, z, core), 1 - core).wait_recv())

        def give(s):
            def plane(i):
                staged[pl.ds(s, 1), pl.ds(h * half + i, 1)] = picked(s, h * half + i)[None]

            loop(half, plane)
            hand_copy(h, s, mine).start()

        others(groups, mine, give)

        def keep(i):
            p_buf[pl.ds(h * half + i, 1), strip(mine)] = picked(mine, h * half + i)

        loop(half, keep)

    events = sorted((d + 1.5 * h, h, d) for h in range(HALVES) for d in range(1, line))
    for i, (when, h, d) in enumerate(events):
        hop(h, d)
        if i == 0:
            for later in range(1, HALVES):
                send_own(later)
        if i == len(events) - 2:
            send_halo(0, 0)
            send_halo(1, 0)
        if i < chunks:
            inject(i)
        if d == line - 1:
            if h == 0:
                own_tile.wait()
                others(groups, mine, lambda s: first_copy(s, s).wait_recv())
            hand(h)

    def lap(buf, t, x0):
        centre = buf[t, pl.ds(x0 + 4, CHUNK)].reshape(CHUNK * ny, nz)
        high = centre.astype(BF16)
        low = (centre - high.astype(F32)).astype(BF16)
        along_z = jnp.dot(
            jnp.concatenate([high, low, high], axis=1), zmat[...], preferred_element_type=F32)
        along_y = []
        for i in range(CHUNK):
            rows = slice(i * ny, (i + 1) * ny)
            stack = jnp.concatenate([high[rows], low[rows], high[rows]], axis=0)
            along_y.append(jnp.dot(ymat[...], stack, preferred_element_type=F32))
        total = along_z.reshape(CHUNK, ny, nz) + jnp.stack(along_y)
        for k in range(1, 5):
            total = total + COEF[k] * (
                buf[t, pl.ds(x0 + 4 + k, CHUNK)] + buf[t, pl.ds(x0 + 4 - k, CHUNK)])
        return total

    count = count_ref[0]
    source_x = source_ref[0, 0] - me * tx

    def drive(t, x0):
        total = lap(u_buf, t, x0)
        parts = []
        for i in range(CHUNK):
            amount = jnp.where(source_x == x0 + i, wave_ref[0, t], 0.0)
            parts.append(total[i] + smask[...] * amount)
        total = jnp.stack(parts)
        if t >= 2:
            total = jnp.where(t < count, total, 0.0)
        return total

    def forward(t, x0):
        own = pl.ds(x0, CHUNK)
        mid = pl.ds(x0 + 4, CHUNK)
        if t == 0:
            total, before = d_buf[0, own], u_old[own]
        else:
            total = drive(t, x0)
            d_buf[t, own] = total
            before = u_old[own] if t == 0 else u_buf[t - 1, mid]
        u_buf[t + 1, mid] = 2.0 * u_buf[t, mid] - before + p_buf[own] * total

    def backward(t, x0):
        own = pl.ds(x0, CHUNK)
        mid = pl.ds(x0 + 4, CHUNK)
        s = STEPS - 1 - t
        total = e_buf[own] if t == 0 else lap(w_buf, t, x0) + inj[s, own]
        now = w_buf[t, mid]
        before = w_buf[t - 1, mid] if s + 1 < 2 else w_old[own]
        new = 2.0 * now - before + p_buf[own] * total
        if s >= 2:
            w_old[own] = jnp.where(s < count, now, before)
            new = jnp.where(s < count, new, now)
        return new

    def adjoint(t, x0):
        w_buf[t + 1, pl.ds(x0 + 4, CHUNK)] = backward(t, x0)

    last = tx - CHUNK
    faces = lambda visit: loop(2, lambda i: visit(i * last))
    inner = lambda visit: loop(chunks - 2, lambda i: visit(CHUNK + i * CHUNK))

    for copy in loads:
        copy.wait()

    def early(x0):
        d_buf[0, pl.ds(x0, CHUNK)] = drive(0, x0)
        e_buf[pl.ds(x0, CHUNK)] = lap(w_buf, 0, x0) + inj[STEPS - 1, pl.ds(x0, CHUNK)]

    inner(early)
    wait_halo(0, 0)
    wait_halo(1, 0)
    faces(early)

    for h in range(HALVES):
        others(groups, mine, lambda s: hand_copy(h, s, s).wait_recv())

    for t in range(STEPS - 1):
        if t:
            wait_halo(0, t)
        faces(functools.partial(forward, t))
        send_halo(0, t + 1)
        inner(functools.partial(forward, t))
        if t:
            wait_halo(1, t)
        faces(functools.partial(adjoint, t))
        send_halo(1, t + 1)
        inner(functools.partial(adjoint, t))

    def image_copy(c, s, sender):
        xs = pl.ds(c * CHUNK, CHUNK)
        return remote(
            img.at[xs, strip(s)], shared.at[sender, xs],
            i_send.at[c, s], i_recv.at[c, sender], {"shot": s})

    def final(x0):
        own = pl.ds(x0, CHUNK)
        mid = pl.ds(x0 + 4, CHUNK)
        t = STEPS - 1
        new = backward(t, x0) * d_buf[0, own]
        new = new + w_buf[1, mid] * drive(t, x0)
        for k in range(1, t):
            new = new + w_buf[k + 1, mid] * d_buf[t - k, own]
        img[own] = new
        c = lax.div(x0, CHUNK)
        others(groups, mine, lambda s: image_copy(c, s, mine).start())
        shared[pl.ds(mine, 1), own] = img[own, strip(mine)].reshape(1, CHUNK, q, nz)

    inner(final)
    wait_halo(0, STEPS - 1)
    wait_halo(1, STEPS - 1)
    faces(final)

    def beside_copy(c):
        xs = pl.ds(c * CHUNK, CHUNK)
        return remote(shared.at[:, xs], beside.at[:, xs], g_send.at[c], g_recv.at[c], {"mp": sibling})

    order = list(range(1, chunks - 1)) + [0, chunks - 1]
    for c in order:
        others(groups, mine, lambda s: image_copy(c, s, s).wait_recv())
        beside_copy(c).start()

    starts = [jnp.max(firsts[s]) for s in range(groups)]

    def sum_copy(r, z, c):
        xs = pl.ds(c * CHUNK, CHUNK)
        return remote(
            part.at[r, z, xs], arrived.at[r, z, xs], o_send.at[r, z, c], o_recv.at[r, z, c],
            {"mp": me + 2 if r == 0 else me - 2})

    def local_sum(r, z, c):
        tile = r * n + 2 * z + core
        xs = pl.ds(c * CHUNK, CHUNK)
        value = jnp.zeros((CHUNK, q, nz), F32)
        for s in range(groups):
            value = value + jnp.where(starts[s] == tile - me, shared[s, xs], 0.0)
            value = value + jnp.where(starts[s] == tile - sibling, beside[s, xs], 0.0)
        return value

    def sourced(r):
        return chip > 0 if r == 0 else chip < line - 1

    for j in range(line - 1):
        for c in order:
            if j == 0:
                beside_copy(c).wait_recv()
            xs = pl.ds(c * CHUNK, CHUNK)
            for r in range(2):
                late = chip if r == 0 else line - 1 - chip
                z = line - 1 - j + chip if r == 0 else j - line + 1 + chip

                @pl.when(late <= j)
                def _():
                    part[r, z, xs] = local_sum(r, z, c)

                    @pl.when(sourced(r))
                    def _():
                        sum_copy(r, z, c).wait_recv()
                        part[r, z, xs] += arrived[r, z, xs]

                    sum_copy(r, z, c).start()

    for c in order:
        xs = pl.ds(c * CHUNK, CHUNK)
        for r in range(2):
            out_ref[r, xs] = local_sum(r, chip, c)

            @pl.when(sourced(r))
            def _():
                sum_copy(r, chip, c).wait_recv()
                out_ref[r, xs] += arrived[r, chip, xs]

    others(groups, mine, lambda s: first_copy(s, mine).wait_send())
    for h in range(HALVES):
        def sent(r, z):
            src = tile_ref(h, r, z, core)
            across(h, r, z, src, core).wait_send()

            @pl.when(onward(r))
            def _():
                along(h, r, z, src).wait_send()

        each_tile(sent)
        others(groups, mine, lambda s: hand_copy(h, s, mine).wait_send())
    for c in range(chunks):
        others(groups, mine, lambda s: image_copy(c, s, mine).wait_send())
        beside_copy(c).wait_send()
        for j in range(line - 1):
            for r in range(2):
                late = chip if r == 0 else line - 1 - chip
                z = line - 1 - j + chip if r == 0 else j - line + 1 + chip

                @pl.when(late <= j)
                def _():
                    sum_copy(r, z, c).wait_send()
    for t in range(STEPS):
        drain_halo(0, t)
        drain_halo(1, t)


def body(
    courant, aperture_first, source_pos, wavelet, receiver_pos, residual, step_count,
    forward_prev, forward_now, adjoint_prev, adjoint_now,
):
    n = lax.axis_size("mp")
    groups = lax.axis_size("shot")
    tx, ny, nz = courant.shape[1:]
    recv = receiver_pos.shape[1]
    q = ny // groups
    line = n // 2
    chunks = tx // CHUNK
    smem = pl.BlockSpec(memory_space=pltpu.SMEM)
    vmem = pl.BlockSpec(memory_space=pltpu.VMEM)
    hbm = pl.BlockSpec(memory_space=pl.ANY)
    dma = pltpu.SemaphoreType.DMA
    return pl.pallas_call(
        functools.partial(kernel, n, groups, tx, ny, nz, recv),
        out_shape=jax.ShapeDtypeStruct((2, tx, q, nz), F32),
        in_specs=[smem] * 4 + [vmem] * 2 + [hbm] * 5,
        out_specs=vmem,
        scratch_shapes=[
            pltpu.VMEM((STEPS, tx + 8, ny, nz), F32),
            pltpu.VMEM((STEPS, tx + 8, ny, nz), F32),
            pltpu.VMEM((tx, ny, nz), F32),
            pltpu.VMEM((tx, ny, nz), F32),
            pltpu.VMEM((tx, ny, nz), F32),
            pltpu.VMEM((STEPS - 1, tx, ny, nz), F32),
            pltpu.VMEM((STEPS, tx, ny, nz), F32),
            pltpu.VMEM((tx, ny, nz), F32),
            pltpu.VMEM((2, n, tx, q, nz), F32),
            pltpu.VMEM((groups, tx, q, nz), F32),
            pltpu.VMEM((tx, ny, nz), F32),
            pltpu.VMEM((groups, tx, q, nz), F32),
            pltpu.VMEM((groups, tx, q, nz), F32),
            pltpu.VMEM((2, line, tx, q, nz), F32),
            pltpu.VMEM((2, line, tx, q, nz), F32),
            pltpu.VMEM((groups, 8, 128), jnp.int32),
            pltpu.VMEM((3 * nz, nz), BF16),
            pltpu.VMEM((ny, 3 * ny), BF16),
            pltpu.VMEM((ny, nz), F32),
            pltpu.VMEM((3 * recv, nz), BF16),
            dma((5,)),
            dma((2, STEPS, 2)), dma((2, STEPS, 2)),
            dma((groups,)), dma((groups,)),
            dma((HALVES, 2, line)), dma((HALVES, 2, line)),
            dma((HALVES, 2, line)), dma((HALVES, 2, line)),
            dma((HALVES, groups)), dma((HALVES, groups)),
            dma((chunks, groups)), dma((chunks, groups)),
            dma((chunks,)), dma((chunks,)),
            dma((2, line, chunks)), dma((2, line, chunks)),
        ],
        compiler_params=pltpu.CompilerParams(
            collective_id=0, has_side_effects=True, vmem_limit_bytes=58 * 1024 * 1024),
    )(
        aperture_first, source_pos, wavelet, step_count,
        receiver_pos.transpose(2, 0, 1), residual,
        courant, forward_prev, forward_now, adjoint_prev, adjoint_now,
    )


def solution(mesh):
    return jax.shard_map(
        body,
        mesh=mesh,
        in_specs=(
            P(None, "mp", None, None),
            P("shot"),
            P("shot", None),
            P("shot", None),
            P("shot", None, None),
            P("shot", None, None),
            P("shot"),
            P("shot", "mp", None, None),
            P("shot", "mp", None, None),
            P("shot", "mp", None, None),
            P("shot", "mp", None, None),
        ),
        out_specs=P(None, "mp", "shot", None),
        check_vma=False,
    )
```

```python
import functools

import jax
import jax.numpy as jnp
from jax import lax
from jax.experimental import pallas as pl
from jax.experimental.pallas import tpu as pltpu
from jax.sharding import PartitionSpec as P

COEF = (-205.0 / 72.0, 1.6, -0.2, 8.0 / 315.0, -1.0 / 560.0)
F32 = jnp.float32
BF16 = jnp.bfloat16
MESH = pl.DeviceIdType.MESH
CHUNK = 4
STEPS = 4
SCALE = 5040.0
OUTER = (8064.0, -1008.0, 128.0, -9.0)


def parts_of(line):
    return 4 if line <= 4 else 2


def band(size):
    row = lax.broadcasted_iota(jnp.int32, (size, size), 0)
    col = lax.broadcasted_iota(jnp.int32, (size, size), 1)
    gap = jnp.abs(row - col)
    value = jnp.zeros((size, size), F32)
    for k in range(1, 5):
        value = jnp.where(gap == k, OUTER[k - 1], value)
    return value.astype(BF16)


def kernel(
    n, groups, tx, ny, nz, recv,
    first_ref, source_ref, wave_ref, count_ref, rec_ref, res_ref,
    courant, fprev, fnow, aprev, anow,
    out_ref,
    u_buf, w_buf, u_old, w_old, e_buf, d_buf, inj, p_buf,
    tiles, staged, img, shared, beside, part, arrived, firsts, zmat, ymat, smask, rmat,
    load_sem, halo_send, halo_recv, f_send, f_recv, a_send, a_recv, b_send, b_recv,
    x_send, x_recv, i_send, i_recv, g_send, g_recv, o_send, o_recv,
):
    me = lax.axis_index("mp")
    mine = lax.axis_index("shot")
    chip, core = lax.div(me, 2), lax.rem(me, 2)
    sibling = me + 1 - 2 * core
    line = n // 2
    q = ny // groups
    chunks = tx // CHUNK
    halves = parts_of(line)
    half = tx // halves

    def strip(s):
        return pl.ds(pl.multiple_of(s * q, q), q)

    def others(count, own, visit):
        def go(o, carry):
            visit(lax.rem(own + o, count))
            return carry

        lax.fori_loop(1, count, go, 0)

    def loop(count, visit):
        def go(o, carry):
            visit(o)
            return carry

        lax.fori_loop(0, count, go, 0)

    def remote(src, dst, send, recv_, target):
        return pltpu.make_async_remote_copy(
            src_ref=src, dst_ref=dst, send_sem=send, recv_sem=recv_,
            device_id=target, device_id_type=MESH,
        )

    barrier = pltpu.get_barrier_semaphore()
    nearby = [(me - 1, me >= 1), (me + 1, me < n - 1), (me - 2, me >= 2), (me + 2, me < n - 2)]
    for k, there in nearby:
        @pl.when(there)
        def _(k=k):
            pl.semaphore_signal(barrier, inc=1, device_id={"mp": k}, device_id_type=MESH)
    others(groups, mine, lambda s: pl.semaphore_signal(
        barrier, inc=1, device_id={"shot": s}, device_id_type=MESH))
    peers = groups - 1 + jnp.minimum(me, 2) + jnp.minimum(n - 1 - me, 2)
    pl.semaphore_wait(barrier, peers)

    def tile_ref(h, r, z, c):
        return tiles.at[r, 2 * z + c, pl.ds(h * half, half)]

    def own_ref(h, r):
        return courant.at[r, pl.ds(h * half, half), strip(mine)]

    def along(h, r, z, src):
        return remote(
            src, tile_ref(h, r, z, core), a_send.at[h, r, z], a_recv.at[h, r, z],
            {"mp": me - 2 if r == 0 else me + 2})

    def across(h, r, z, src, c):
        return remote(
            src, tile_ref(h, r, z, c), b_send.at[h, r, z], b_recv.at[h, r, z], {"mp": sibling})

    def onward(r):
        return chip > 0 if r == 0 else chip < line - 1

    def send_own(h):
        for r in range(2):
            @pl.when(onward(r))
            def _():
                along(h, r, chip, own_ref(h, r)).start()
        for r in range(2):
            across(h, r, chip, own_ref(h, r), core).start()

    def hop(h, d):
        for r in range(2):
            z = chip + d if r == 0 else chip - d
            there = z < line if r == 0 else z >= 0

            @pl.when(there)
            def _():
                along(h, r, z, tile_ref(h, r, z, core)).wait_recv()

                @pl.when(onward(r))
                def _():
                    along(h, r, z, tile_ref(h, r, z, core)).start()

                across(h, r, z, tile_ref(h, r, z, core), core).start()

    def each_tile(visit):
        for d in range(line):
            for r in range(2):
                z = chip + d if r == 0 else chip - d

                @pl.when(z < line if r == 0 else z >= 0)
                def _():
                    visit(r, z)

    def first_copy(s, sender):
        return remote(firsts.at[sender], firsts.at[sender], f_send.at[s], f_recv.at[sender], {"shot": s})

    send_own(0)
    firsts[pl.ds(mine, 1)] = jnp.full((1, 8, 128), first_ref[0], jnp.int32)
    others(groups, mine, lambda s: first_copy(s, mine).start())
    own_tile = pltpu.make_async_copy(courant.at[:, :, strip(mine)], tiles.at[:, me], load_sem.at[4])
    own_tile.start()

    def halo(f, t, side, src):
        buf = (u_buf, w_buf)[f]
        dst = buf.at[t, pl.ds(0, 4)] if side == 0 else buf.at[t, pl.ds(tx + 4, 4)]
        target = me + 1 if side == 0 else me - 1
        return remote(src, dst, halo_send.at[f, t, side], halo_recv.at[f, t, side], {"mp": target})

    def halo_src(f, t, side):
        if t == 0:
            src = (fnow, anow)[f]
            return src.at[0, pl.ds(tx - 4, 4)] if side == 0 else src.at[0, pl.ds(0, 4)]
        buf = (u_buf, w_buf)[f]
        return buf.at[t, pl.ds(tx, 4)] if side == 0 else buf.at[t, pl.ds(4, 4)]

    def send_halo(f, t):
        @pl.when(me < n - 1)
        def _():
            halo(f, t, 0, halo_src(f, t, 0)).start()

        @pl.when(me > 0)
        def _():
            halo(f, t, 1, halo_src(f, t, 1)).start()

    def wait_halo(f, t):
        @pl.when(me > 0)
        def _():
            halo(f, t, 0, halo_src(f, t, 0)).wait_recv()

        @pl.when(me < n - 1)
        def _():
            halo(f, t, 1, halo_src(f, t, 1)).wait_recv()

    def drain_halo(f, t):
        @pl.when(me < n - 1)
        def _():
            halo(f, t, 0, halo_src(f, t, 0)).wait_send()

        @pl.when(me > 0)
        def _():
            halo(f, t, 1, halo_src(f, t, 1)).wait_send()

    loads = [
        pltpu.make_async_copy(fnow.at[0], u_buf.at[0, pl.ds(4, tx)], load_sem.at[0]),
        pltpu.make_async_copy(anow.at[0], w_buf.at[0, pl.ds(4, tx)], load_sem.at[1]),
        pltpu.make_async_copy(fprev.at[0], u_old, load_sem.at[2]),
        pltpu.make_async_copy(aprev.at[0], w_old, load_sem.at[3]),
    ]
    for copy in loads:
        copy.start()

    edge = jnp.zeros((4, ny, nz), F32)

    @pl.when(me == 0)
    def _():
        for t in range(STEPS):
            u_buf[t, pl.ds(0, 4)] = edge
            w_buf[t, pl.ds(0, 4)] = edge

    @pl.when(me == n - 1)
    def _():
        for t in range(STEPS):
            u_buf[t, pl.ds(tx + 4, 4)] = edge
            w_buf[t, pl.ds(tx + 4, 4)] = edge

    band_z, band_y = band(nz), band(ny)
    zmat[pl.ds(0, nz)] = band_z
    zmat[pl.ds(nz, nz)] = band_z
    blank = jnp.zeros((ny, 2 * ny), BF16)
    pair = jnp.concatenate([band_y, band_y], axis=1)
    ymat[pl.ds(0, ny)] = jnp.concatenate([pair, blank], axis=1)
    ymat[pl.ds(ny, ny)] = jnp.concatenate([blank, pair], axis=1)
    y_id = lax.broadcasted_iota(jnp.int32, (ny, nz), 0)
    z_id = lax.broadcasted_iota(jnp.int32, (ny, nz), 1)
    smask[...] = jnp.where((y_id == source_ref[0, 1]) & (z_id == source_ref[0, 2]), 1.0, 0.0)
    same = (lax.broadcasted_iota(jnp.int32, (recv, recv), 0)
            == lax.broadcasted_iota(jnp.int32, (recv, recv), 1))
    at_z = jnp.sum(jnp.where(same, rec_ref[2].astype(F32), 0.0), axis=1, keepdims=True)
    hit_z = at_z.astype(jnp.int32) == lax.broadcasted_iota(jnp.int32, (recv, nz), 1)
    hit_z = jnp.where(hit_z, 1.0, 0.0).astype(BF16)
    for i in range(3):
        rmat[pl.ds(i * recv, recv)] = hit_z
    res = res_ref[0]
    res0 = res.astype(BF16).astype(F32)
    res1 = (res - res0).astype(BF16).astype(F32)
    res2 = res - res0 - res1
    res_all = jnp.concatenate([res0, res1, res2], axis=1)
    rec_x = jnp.concatenate([rec_ref[0]] * 3, axis=1)
    rec_y = jnp.concatenate([rec_ref[1]] * 3, axis=1)
    hit_y = lax.broadcasted_iota(jnp.int32, (ny, 3 * recv), 0) == rec_y
    hit_y = jnp.where(hit_y, 1.0, 0.0)

    def inject(c):
        x0 = c * CHUNK
        for s in range(STEPS):
            rows = []
            for i in range(CHUNK):
                at_x = jnp.where(rec_x == me * tx + x0 + i, res_all[s:s + 1], 0.0)
                rows.append((hit_y * at_x).astype(BF16))
            field = jnp.dot(jnp.concatenate(rows, axis=0), rmat[...], preferred_element_type=F32)
            inj[s, pl.ds(x0, CHUNK)] = field.reshape(CHUNK, ny, nz)

    def hand_copy(h, s, sender):
        xs = pl.ds(h * half, half)
        return remote(
            staged.at[s, xs], p_buf.at[xs, strip(sender)],
            x_send.at[h, s], x_recv.at[h, sender], {"shot": s})

    def picked(s, x):
        first = jnp.max(firsts[pl.ds(s, 1)])
        value = jnp.zeros((1, q, nz), F32)
        for k in range(n + 1):
            t = me + k
            value = jnp.where(first == k, tiles[lax.div(t, n), lax.rem(t, n), pl.ds(x, 1)], value)
        return value

    def hand(h):
        each_tile(lambda r, z: across(h, r, z, tile_ref(h, r, z, core), 1 - core).wait_recv())

        def give(s):
            def plane(i):
                staged[pl.ds(s, 1), pl.ds(h * half + i, 1)] = picked(s, h * half + i)[None]

            loop(half, plane)
            hand_copy(h, s, mine).start()

        others(groups, mine, give)

        def keep(i):
            p_buf[pl.ds(h * half + i, 1), strip(mine)] = picked(mine, h * half + i)

        loop(half, keep)

    events = sorted((d + (1 + halves / 4) * h, h, d) for h in range(halves) for d in range(1, line))
    for i, (when, h, d) in enumerate(events):
        hop(h, d)
        if d == 1 and h + 1 < halves:
            send_own(h + 1)
        if i == len(events) - 2:
            send_halo(0, 0)
            send_halo(1, 0)
        if i < chunks:
            inject(i)
        if d == line - 1:
            if h == 0:
                own_tile.wait()
                others(groups, mine, lambda s: first_copy(s, s).wait_recv())
            hand(h)

    def lap(buf, t, x0):
        centre = buf[t, pl.ds(x0 + 4, CHUNK)].reshape(CHUNK * ny, nz)
        high = centre.astype(BF16)
        low = (centre - high.astype(F32)).astype(BF16)
        outer = jnp.dot(
            jnp.concatenate([high, low], axis=1), zmat[...], preferred_element_type=F32)
        along_y = []
        for i in range(0, CHUNK, 2):
            one, two = slice(i * ny, (i + 1) * ny), slice((i + 1) * ny, (i + 2) * ny)
            stack = jnp.concatenate([high[one], low[one], high[two], low[two]], axis=0)
            along_y.append(jnp.dot(ymat[...], stack, preferred_element_type=F32))
        outer = outer + jnp.concatenate(along_y, axis=0)
        total = (outer * (1.0 / SCALE) + 3.0 * COEF[0] * centre).reshape(CHUNK, ny, nz)
        for k in range(1, 5):
            total = total + COEF[k] * (
                buf[t, pl.ds(x0 + 4 + k, CHUNK)] + buf[t, pl.ds(x0 + 4 - k, CHUNK)])
        return total

    count = count_ref[0]
    source_x = source_ref[0, 0] - me * tx

    def drive(t, x0):
        total = lap(u_buf, t, x0)
        parts = []
        for i in range(CHUNK):
            amount = jnp.where(source_x == x0 + i, wave_ref[0, t], 0.0)
            parts.append(total[i] + smask[...] * amount)
        total = jnp.stack(parts)
        if t >= 2:
            total = jnp.where(t < count, total, 0.0)
        return total

    def forward(t, x0):
        own = pl.ds(x0, CHUNK)
        mid = pl.ds(x0 + 4, CHUNK)
        if t == 0:
            total, before = d_buf[0, own], u_old[own]
        else:
            total = drive(t, x0)
            d_buf[t, own] = total
            before = u_old[own] if t == 0 else u_buf[t - 1, mid]
        u_buf[t + 1, mid] = 2.0 * u_buf[t, mid] - before + p_buf[own] * total

    def backward(t, x0):
        own = pl.ds(x0, CHUNK)
        mid = pl.ds(x0 + 4, CHUNK)
        s = STEPS - 1 - t
        total = e_buf[own] if t == 0 else lap(w_buf, t, x0) + inj[s, own]
        now = w_buf[t, mid]
        before = w_buf[t - 1, mid] if s + 1 < 2 else w_old[own]
        new = 2.0 * now - before + p_buf[own] * total
        if s >= 2:
            w_old[own] = jnp.where(s < count, now, before)
            new = jnp.where(s < count, new, now)
        return new

    def adjoint(t, x0):
        w_buf[t + 1, pl.ds(x0 + 4, CHUNK)] = backward(t, x0)

    last = tx - CHUNK
    faces = lambda visit: loop(2, lambda i: visit(i * last))
    inner = lambda visit: loop(chunks - 2, lambda i: visit(CHUNK + i * CHUNK))

    for copy in loads:
        copy.wait()

    def early(x0):
        d_buf[0, pl.ds(x0, CHUNK)] = drive(0, x0)
        e_buf[pl.ds(x0, CHUNK)] = lap(w_buf, 0, x0) + inj[STEPS - 1, pl.ds(x0, CHUNK)]

    inner(early)
    wait_halo(0, 0)
    wait_halo(1, 0)
    faces(early)

    for h in range(halves):
        others(groups, mine, lambda s: hand_copy(h, s, s).wait_recv())

    for t in range(STEPS - 1):
        if t:
            wait_halo(0, t)
        faces(functools.partial(forward, t))
        send_halo(0, t + 1)
        inner(functools.partial(forward, t))
        if t:
            wait_halo(1, t)
        faces(functools.partial(adjoint, t))
        send_halo(1, t + 1)
        inner(functools.partial(adjoint, t))

    def image_copy(c, s, sender):
        xs = pl.ds(c * CHUNK, CHUNK)
        return remote(
            img.at[xs, strip(s)], shared.at[sender, xs],
            i_send.at[c, s], i_recv.at[c, sender], {"shot": s})

    def final(x0):
        own = pl.ds(x0, CHUNK)
        mid = pl.ds(x0 + 4, CHUNK)
        t = STEPS - 1
        new = backward(t, x0) * d_buf[0, own]
        new = new + w_buf[1, mid] * drive(t, x0)
        for k in range(1, t):
            new = new + w_buf[k + 1, mid] * d_buf[t - k, own]
        img[own] = new
        c = lax.div(x0, CHUNK)
        others(groups, mine, lambda s: image_copy(c, s, mine).start())
        shared[pl.ds(mine, 1), own] = img[own, strip(mine)].reshape(1, CHUNK, q, nz)

    inner(final)
    wait_halo(0, STEPS - 1)
    wait_halo(1, STEPS - 1)
    faces(final)

    def beside_copy(c):
        xs = pl.ds(c * CHUNK, CHUNK)
        return remote(shared.at[:, xs], beside.at[:, xs], g_send.at[c], g_recv.at[c], {"mp": sibling})

    order = list(range(1, chunks - 1)) + [0, chunks - 1]
    starts = [jnp.max(firsts[s]) for s in range(groups)]

    def sum_copy(r, z, c):
        xs = pl.ds(c * CHUNK, CHUNK)
        return remote(
            part.at[r, z, xs], arrived.at[r, z, xs], o_send.at[r, z, c], o_recv.at[r, z, c],
            {"mp": me + 2 if r == 0 else me - 2})

    def local_sum(r, z, c):
        tile = r * n + 2 * z + core
        xs = pl.ds(c * CHUNK, CHUNK)
        value = jnp.zeros((CHUNK, q, nz), F32)
        for s in range(groups):
            value = value + jnp.where(starts[s] == tile - me, shared[s, xs], 0.0)
            value = value + jnp.where(starts[s] == tile - sibling, beside[s, xs], 0.0)
        return value

    def sourced(r):
        return chip > 0 if r == 0 else chip < line - 1

    for c in order:
        others(groups, mine, lambda s: image_copy(c, s, s).wait_recv())
        beside_copy(c).start()
        beside_copy(c).wait_recv()
        xs = pl.ds(c * CHUNK, CHUNK)
        for j in range(line - 1):
            for r in range(2):
                late = chip if r == 0 else line - 1 - chip
                z = line - 1 - j + chip if r == 0 else j - line + 1 + chip

                @pl.when(late <= j)
                def _():
                    part[r, z, xs] = local_sum(r, z, c)

                    @pl.when(sourced(r))
                    def _():
                        sum_copy(r, z, c).wait_recv()
                        part[r, z, xs] += arrived[r, z, xs]

                    sum_copy(r, z, c).start()
        for r in range(2):
            out_ref[r, xs] = local_sum(r, chip, c)

    for c in order:
        xs = pl.ds(c * CHUNK, CHUNK)
        for r in range(2):
            @pl.when(sourced(r))
            def _():
                sum_copy(r, chip, c).wait_recv()
                out_ref[r, xs] += arrived[r, chip, xs]

    others(groups, mine, lambda s: first_copy(s, mine).wait_send())
    for h in range(halves):
        def sent(r, z):
            src = tile_ref(h, r, z, core)
            across(h, r, z, src, core).wait_send()

            @pl.when(onward(r))
            def _():
                along(h, r, z, src).wait_send()

        each_tile(sent)
        others(groups, mine, lambda s: hand_copy(h, s, mine).wait_send())
    for c in range(chunks):
        others(groups, mine, lambda s: image_copy(c, s, mine).wait_send())
        beside_copy(c).wait_send()
        for j in range(line - 1):
            for r in range(2):
                late = chip if r == 0 else line - 1 - chip
                z = line - 1 - j + chip if r == 0 else j - line + 1 + chip

                @pl.when(late <= j)
                def _():
                    sum_copy(r, z, c).wait_send()
    for t in range(STEPS):
        drain_halo(0, t)
        drain_halo(1, t)


def body(
    courant, aperture_first, source_pos, wavelet, receiver_pos, residual, step_count,
    forward_prev, forward_now, adjoint_prev, adjoint_now,
):
    n = lax.axis_size("mp")
    groups = lax.axis_size("shot")
    tx, ny, nz = courant.shape[1:]
    recv = receiver_pos.shape[1]
    q = ny // groups
    line = n // 2
    halves = parts_of(line)
    chunks = tx // CHUNK
    smem = pl.BlockSpec(memory_space=pltpu.SMEM)
    vmem = pl.BlockSpec(memory_space=pltpu.VMEM)
    hbm = pl.BlockSpec(memory_space=pl.ANY)
    dma = pltpu.SemaphoreType.DMA
    return pl.pallas_call(
        functools.partial(kernel, n, groups, tx, ny, nz, recv),
        out_shape=jax.ShapeDtypeStruct((2, tx, q, nz), F32),
        in_specs=[smem] * 4 + [vmem] * 2 + [hbm] * 5,
        out_specs=vmem,
        scratch_shapes=[
            pltpu.VMEM((STEPS, tx + 8, ny, nz), F32),
            pltpu.VMEM((STEPS, tx + 8, ny, nz), F32),
            pltpu.VMEM((tx, ny, nz), F32),
            pltpu.VMEM((tx, ny, nz), F32),
            pltpu.VMEM((tx, ny, nz), F32),
            pltpu.VMEM((STEPS - 1, tx, ny, nz), F32),
            pltpu.VMEM((STEPS, tx, ny, nz), F32),
            pltpu.VMEM((tx, ny, nz), F32),
            pltpu.VMEM((2, n, tx, q, nz), F32),
            pltpu.VMEM((groups, tx, q, nz), F32),
            pltpu.VMEM((tx, ny, nz), F32),
            pltpu.VMEM((groups, tx, q, nz), F32),
            pltpu.VMEM((groups, tx, q, nz), F32),
            pltpu.VMEM((2, line, tx, q, nz), F32),
            pltpu.VMEM((2, line, tx, q, nz), F32),
            pltpu.VMEM((groups, 8, 128), jnp.int32),
            pltpu.VMEM((2 * nz, nz), BF16),
            pltpu.VMEM((2 * ny, 4 * ny), BF16),
            pltpu.VMEM((ny, nz), F32),
            pltpu.VMEM((3 * recv, nz), BF16),
            dma((5,)),
            dma((2, STEPS, 2)), dma((2, STEPS, 2)),
            dma((groups,)), dma((groups,)),
            dma((halves, 2, line)), dma((halves, 2, line)),
            dma((halves, 2, line)), dma((halves, 2, line)),
            dma((halves, groups)), dma((halves, groups)),
            dma((chunks, groups)), dma((chunks, groups)),
            dma((chunks,)), dma((chunks,)),
            dma((2, line, chunks)), dma((2, line, chunks)),
        ],
        compiler_params=pltpu.CompilerParams(
            collective_id=0, has_side_effects=True, vmem_limit_bytes=58 * 1024 * 1024),
    )(
        aperture_first, source_pos, wavelet, step_count,
        receiver_pos.transpose(2, 0, 1), residual,
        courant, forward_prev, forward_now, adjoint_prev, adjoint_now,
    )


def solution(mesh):
    return jax.shard_map(
        body,
        mesh=mesh,
        in_specs=(
            P(None, "mp", None, None),
            P("shot"),
            P("shot", None),
            P("shot", None),
            P("shot", None, None),
            P("shot", None, None),
            P("shot"),
            P("shot", "mp", None, None),
            P("shot", "mp", None, None),
            P("shot", "mp", None, None),
            P("shot", "mp", None, None),
        ),
        out_specs=P(None, "mp", "shot", None),
        check_vma=False,
    )
```

```python
import functools

import jax
import jax.numpy as jnp
from jax import lax
from jax.experimental import pallas as pl
from jax.experimental.pallas import tpu as pltpu
from jax.sharding import PartitionSpec as P

COEF = (-205.0 / 72.0, 1.6, -0.2, 8.0 / 315.0, -1.0 / 560.0)
F32 = jnp.float32
BF16 = jnp.bfloat16
MESH = pl.DeviceIdType.MESH
CHUNK = 4
STEPS = 4
SCALE = 5040.0
OUTER = (8064.0, -1008.0, 128.0, -9.0)


def parts_of(line):
    return 4 if line <= 4 else 2


def band(size):
    row = lax.broadcasted_iota(jnp.int32, (size, size), 0)
    col = lax.broadcasted_iota(jnp.int32, (size, size), 1)
    gap = jnp.abs(row - col)
    value = jnp.zeros((size, size), F32)
    for k in range(1, 5):
        value = jnp.where(gap == k, OUTER[k - 1], value)
    return value.astype(BF16)


def kernel(
    n, groups, tx, ny, nz, recv,
    first_ref, source_ref, wave_ref, count_ref, rec_ref, res_ref,
    courant, fprev, fnow, aprev, anow,
    out_ref,
    u_buf, w_buf, u_old, w_old, e_buf, d_buf, inj, p_buf,
    tiles, staged, img, shared, beside, part, arrived, firsts, zmat, ymat, smask, rmat,
    load_sem, halo_send, halo_recv, f_send, f_recv, a_send, a_recv, b_send, b_recv,
    x_send, x_recv, i_send, i_recv, g_send, g_recv, o_send, o_recv,
):
    me = lax.axis_index("mp")
    mine = lax.axis_index("shot")
    chip, core = lax.div(me, 2), lax.rem(me, 2)
    sibling = me + 1 - 2 * core
    line = n // 2
    q = ny // groups
    chunks = tx // CHUNK
    halves = parts_of(line)
    half = tx // halves

    def strip(s):
        return pl.ds(pl.multiple_of(s * q, q), q)

    def others(count, own, visit):
        def go(o, carry):
            visit(lax.rem(own + o, count))
            return carry

        lax.fori_loop(1, count, go, 0)

    def loop(count, visit):
        def go(o, carry):
            visit(o)
            return carry

        lax.fori_loop(0, count, go, 0)

    def remote(src, dst, send, recv_, target):
        return pltpu.make_async_remote_copy(
            src_ref=src, dst_ref=dst, send_sem=send, recv_sem=recv_,
            device_id=target, device_id_type=MESH,
        )

    barrier = pltpu.get_barrier_semaphore()
    nearby = [(me - 1, me >= 1), (me + 1, me < n - 1), (me - 2, me >= 2), (me + 2, me < n - 2)]
    for k, there in nearby:
        @pl.when(there)
        def _(k=k):
            pl.semaphore_signal(barrier, inc=1, device_id={"mp": k}, device_id_type=MESH)
    others(groups, mine, lambda s: pl.semaphore_signal(
        barrier, inc=1, device_id={"shot": s}, device_id_type=MESH))
    peers = groups - 1 + jnp.minimum(me, 2) + jnp.minimum(n - 1 - me, 2)
    pl.semaphore_wait(barrier, peers)

    def tile_ref(h, r, z, c):
        return tiles.at[r, 2 * z + c, pl.ds(h * half, half)]

    def own_ref(h, r):
        return courant.at[r, pl.ds(h * half, half), strip(mine)]

    def along(h, r, z, src):
        return remote(
            src, tile_ref(h, r, z, core), a_send.at[h, r, z], a_recv.at[h, r, z],
            {"mp": me - 2 if r == 0 else me + 2})

    def across(h, r, z, src, c):
        return remote(
            src, tile_ref(h, r, z, c), b_send.at[h, r, z], b_recv.at[h, r, z], {"mp": sibling})

    def onward(r):
        return chip > 0 if r == 0 else chip < line - 1

    def send_own(h):
        for r in range(2):
            @pl.when(onward(r))
            def _():
                along(h, r, chip, own_ref(h, r)).start()
        for r in range(2):
            across(h, r, chip, own_ref(h, r), core).start()

    def hop(h, d):
        for r in range(2):
            z = chip + d if r == 0 else chip - d
            there = z < line if r == 0 else z >= 0

            @pl.when(there)
            def _():
                along(h, r, z, tile_ref(h, r, z, core)).wait_recv()

                @pl.when(onward(r))
                def _():
                    along(h, r, z, tile_ref(h, r, z, core)).start()

                across(h, r, z, tile_ref(h, r, z, core), core).start()

    def each_tile(visit):
        for d in range(line):
            for r in range(2):
                z = chip + d if r == 0 else chip - d

                @pl.when(z < line if r == 0 else z >= 0)
                def _():
                    visit(r, z)

    def first_copy(s, sender):
        return remote(firsts.at[sender], firsts.at[sender], f_send.at[s], f_recv.at[sender], {"shot": s})

    send_own(0)
    firsts[pl.ds(mine, 1)] = jnp.full((1, 8, 128), first_ref[0], jnp.int32)
    others(groups, mine, lambda s: first_copy(s, mine).start())
    own_tile = pltpu.make_async_copy(courant.at[:, :, strip(mine)], tiles.at[:, me], load_sem.at[4])
    own_tile.start()

    def halo(f, t, side, src):
        buf = (u_buf, w_buf)[f]
        dst = buf.at[t, pl.ds(0, 4)] if side == 0 else buf.at[t, pl.ds(tx + 4, 4)]
        target = me + 1 if side == 0 else me - 1
        return remote(src, dst, halo_send.at[f, t, side], halo_recv.at[f, t, side], {"mp": target})

    def halo_src(f, t, side):
        if t == 0:
            src = (fnow, anow)[f]
            return src.at[0, pl.ds(tx - 4, 4)] if side == 0 else src.at[0, pl.ds(0, 4)]
        buf = (u_buf, w_buf)[f]
        return buf.at[t, pl.ds(tx, 4)] if side == 0 else buf.at[t, pl.ds(4, 4)]

    def send_halo(f, t):
        @pl.when(me < n - 1)
        def _():
            halo(f, t, 0, halo_src(f, t, 0)).start()

        @pl.when(me > 0)
        def _():
            halo(f, t, 1, halo_src(f, t, 1)).start()

    def wait_halo(f, t):
        @pl.when(me > 0)
        def _():
            halo(f, t, 0, halo_src(f, t, 0)).wait_recv()

        @pl.when(me < n - 1)
        def _():
            halo(f, t, 1, halo_src(f, t, 1)).wait_recv()

    def drain_halo(f, t):
        @pl.when(me < n - 1)
        def _():
            halo(f, t, 0, halo_src(f, t, 0)).wait_send()

        @pl.when(me > 0)
        def _():
            halo(f, t, 1, halo_src(f, t, 1)).wait_send()

    loads = [
        pltpu.make_async_copy(fnow.at[0], u_buf.at[0, pl.ds(4, tx)], load_sem.at[0]),
        pltpu.make_async_copy(anow.at[0], w_buf.at[0, pl.ds(4, tx)], load_sem.at[1]),
        pltpu.make_async_copy(fprev.at[0], u_old, load_sem.at[2]),
        pltpu.make_async_copy(aprev.at[0], w_old, load_sem.at[3]),
    ]
    for copy in loads:
        copy.start()

    edge = jnp.zeros((4, ny, nz), F32)

    @pl.when(me == 0)
    def _():
        for t in range(STEPS):
            u_buf[t, pl.ds(0, 4)] = edge
            w_buf[t, pl.ds(0, 4)] = edge

    @pl.when(me == n - 1)
    def _():
        for t in range(STEPS):
            u_buf[t, pl.ds(tx + 4, 4)] = edge
            w_buf[t, pl.ds(tx + 4, 4)] = edge

    band_z, band_y = band(nz), band(ny)
    zmat[pl.ds(0, nz)] = band_z
    zmat[pl.ds(nz, nz)] = band_z
    blank = jnp.zeros((ny, 2 * ny), BF16)
    pair = jnp.concatenate([band_y, band_y], axis=1)
    ymat[pl.ds(0, ny)] = jnp.concatenate([pair, blank], axis=1)
    ymat[pl.ds(ny, ny)] = jnp.concatenate([blank, pair], axis=1)
    y_id = lax.broadcasted_iota(jnp.int32, (ny, nz), 0)
    z_id = lax.broadcasted_iota(jnp.int32, (ny, nz), 1)
    smask[...] = jnp.where((y_id == source_ref[0, 1]) & (z_id == source_ref[0, 2]), 1.0, 0.0)
    same = (lax.broadcasted_iota(jnp.int32, (recv, recv), 0)
            == lax.broadcasted_iota(jnp.int32, (recv, recv), 1))
    at_z = jnp.sum(jnp.where(same, rec_ref[2].astype(F32), 0.0), axis=1, keepdims=True)
    hit_z = at_z.astype(jnp.int32) == lax.broadcasted_iota(jnp.int32, (recv, nz), 1)
    hit_z = jnp.where(hit_z, 1.0, 0.0).astype(BF16)
    for i in range(3):
        rmat[pl.ds(i * recv, recv)] = hit_z
    res = res_ref[0]
    res0 = res.astype(BF16).astype(F32)
    res1 = (res - res0).astype(BF16).astype(F32)
    res2 = res - res0 - res1
    res_all = jnp.concatenate([res0, res1, res2], axis=1)
    rec_x = jnp.concatenate([rec_ref[0]] * 3, axis=1)
    rec_y = jnp.concatenate([rec_ref[1]] * 3, axis=1)
    hit_y = lax.broadcasted_iota(jnp.int32, (ny, 3 * recv), 0) == rec_y
    hit_y = jnp.where(hit_y, 1.0, 0.0)

    def inject(c):
        x0 = c * CHUNK
        for s in range(STEPS):
            rows = []
            for i in range(CHUNK):
                at_x = jnp.where(rec_x == me * tx + x0 + i, res_all[s:s + 1], 0.0)
                rows.append((hit_y * at_x).astype(BF16))
            field = jnp.dot(jnp.concatenate(rows, axis=0), rmat[...], preferred_element_type=F32)
            inj[s, pl.ds(x0, CHUNK)] = field.reshape(CHUNK, ny, nz)

    def hand_copy(h, s, sender):
        xs = pl.ds(h * half, half)
        return remote(
            staged.at[s, xs], p_buf.at[xs, strip(sender)],
            x_send.at[h, s], x_recv.at[h, sender], {"shot": s})

    def picked(s, x):
        first = jnp.max(firsts[pl.ds(s, 1)])
        value = jnp.zeros((1, q, nz), F32)
        for k in range(n + 1):
            t = me + k
            value = jnp.where(first == k, tiles[lax.div(t, n), lax.rem(t, n), pl.ds(x, 1)], value)
        return value

    def hand(h):
        each_tile(lambda r, z: across(h, r, z, tile_ref(h, r, z, core), 1 - core).wait_recv())

        def give(s):
            def plane(i):
                staged[pl.ds(s, 1), pl.ds(h * half + i, 1)] = picked(s, h * half + i)[None]

            loop(half, plane)
            hand_copy(h, s, mine).start()

        others(groups, mine, give)

        def keep(i):
            p_buf[pl.ds(h * half + i, 1), strip(mine)] = picked(mine, h * half + i)

        loop(half, keep)

    for h in range(1, min(2, halves)):
        send_own(h)
    levels = halves + line - 2
    for level in range(1, levels + 1):
        for h in range(halves):
            if 1 <= level - h < line:
                hop(h, level - h)
        if level + 1 < halves:
            send_own(level + 1)
        if level == levels - 1:
            send_halo(0, 0)
            send_halo(1, 0)
        if level <= chunks:
            inject(level - 1)
        h = level - line + 1
        if h == 0:
            own_tile.wait()
            others(groups, mine, lambda s: first_copy(s, s).wait_recv())
        if h >= 0:
            hand(h)

    def lap(buf, t, x0):
        centre = buf[t, pl.ds(x0 + 4, CHUNK)].reshape(CHUNK * ny, nz)
        high = centre.astype(BF16)
        low = (centre - high.astype(F32)).astype(BF16)
        outer = jnp.dot(
            jnp.concatenate([high, low], axis=1), zmat[...], preferred_element_type=F32)
        along_y = []
        for i in range(0, CHUNK, 2):
            one, two = slice(i * ny, (i + 1) * ny), slice((i + 1) * ny, (i + 2) * ny)
            stack = jnp.concatenate([high[one], low[one], high[two], low[two]], axis=0)
            along_y.append(jnp.dot(ymat[...], stack, preferred_element_type=F32))
        outer = outer + jnp.concatenate(along_y, axis=0)
        total = (outer * (1.0 / SCALE) + 3.0 * COEF[0] * centre).reshape(CHUNK, ny, nz)
        for k in range(1, 5):
            total = total + COEF[k] * (
                buf[t, pl.ds(x0 + 4 + k, CHUNK)] + buf[t, pl.ds(x0 + 4 - k, CHUNK)])
        return total

    count = count_ref[0]
    source_x = source_ref[0, 0] - me * tx

    def drive(t, x0):
        total = lap(u_buf, t, x0)
        parts = []
        for i in range(CHUNK):
            amount = jnp.where(source_x == x0 + i, wave_ref[0, t], 0.0)
            parts.append(total[i] + smask[...] * amount)
        total = jnp.stack(parts)
        if t >= 2:
            total = jnp.where(t < count, total, 0.0)
        return total

    def forward(t, x0):
        own = pl.ds(x0, CHUNK)
        mid = pl.ds(x0 + 4, CHUNK)
        if t == 0:
            total, before = d_buf[0, own], u_old[own]
        else:
            total = drive(t, x0)
            d_buf[t, own] = total
            before = u_old[own] if t == 0 else u_buf[t - 1, mid]
        u_buf[t + 1, mid] = 2.0 * u_buf[t, mid] - before + p_buf[own] * total

    def backward(t, x0):
        own = pl.ds(x0, CHUNK)
        mid = pl.ds(x0 + 4, CHUNK)
        s = STEPS - 1 - t
        total = e_buf[own] if t == 0 else lap(w_buf, t, x0) + inj[s, own]
        now = w_buf[t, mid]
        before = w_buf[t - 1, mid] if s + 1 < 2 else w_old[own]
        new = 2.0 * now - before + p_buf[own] * total
        if s >= 2:
            w_old[own] = jnp.where(s < count, now, before)
            new = jnp.where(s < count, new, now)
        return new

    def adjoint(t, x0):
        w_buf[t + 1, pl.ds(x0 + 4, CHUNK)] = backward(t, x0)

    last = tx - CHUNK
    faces = lambda visit: loop(2, lambda i: visit(i * last))
    inner = lambda visit: loop(chunks - 2, lambda i: visit(CHUNK + i * CHUNK))

    for copy in loads:
        copy.wait()

    def early(x0):
        d_buf[0, pl.ds(x0, CHUNK)] = drive(0, x0)
        e_buf[pl.ds(x0, CHUNK)] = lap(w_buf, 0, x0) + inj[STEPS - 1, pl.ds(x0, CHUNK)]

    inner(early)
    wait_halo(0, 0)
    wait_halo(1, 0)
    faces(early)

    for h in range(halves):
        others(groups, mine, lambda s: hand_copy(h, s, s).wait_recv())

    for t in range(STEPS - 1):
        if t:
            wait_halo(0, t)
        faces(functools.partial(forward, t))
        send_halo(0, t + 1)
        inner(functools.partial(forward, t))
        if t:
            wait_halo(1, t)
        faces(functools.partial(adjoint, t))
        send_halo(1, t + 1)
        inner(functools.partial(adjoint, t))

    def image_copy(c, s, sender):
        xs = pl.ds(c * CHUNK, CHUNK)
        return remote(
            img.at[xs, strip(s)], shared.at[sender, xs],
            i_send.at[c, s], i_recv.at[c, sender], {"shot": s})

    def final(x0):
        own = pl.ds(x0, CHUNK)
        mid = pl.ds(x0 + 4, CHUNK)
        t = STEPS - 1
        new = backward(t, x0) * d_buf[0, own]
        new = new + w_buf[1, mid] * drive(t, x0)
        for k in range(1, t):
            new = new + w_buf[k + 1, mid] * d_buf[t - k, own]
        img[own] = new
        c = lax.div(x0, CHUNK)
        others(groups, mine, lambda s: image_copy(c, s, mine).start())
        shared[pl.ds(mine, 1), own] = img[own, strip(mine)].reshape(1, CHUNK, q, nz)

    inner(final)
    wait_halo(0, STEPS - 1)
    wait_halo(1, STEPS - 1)
    faces(final)

    def beside_copy(c):
        xs = pl.ds(c * CHUNK, CHUNK)
        return remote(shared.at[:, xs], beside.at[:, xs], g_send.at[c], g_recv.at[c], {"mp": sibling})

    order = list(range(1, chunks - 1)) + [0, chunks - 1]
    starts = [jnp.max(firsts[s]) for s in range(groups)]

    def sum_copy(r, z, c):
        xs = pl.ds(c * CHUNK, CHUNK)
        return remote(
            part.at[r, z, xs], arrived.at[r, z, xs], o_send.at[r, z, c], o_recv.at[r, z, c],
            {"mp": me + 2 if r == 0 else me - 2})

    def local_sum(r, z, c):
        tile = r * n + 2 * z + core
        xs = pl.ds(c * CHUNK, CHUNK)
        value = jnp.zeros((CHUNK, q, nz), F32)
        for s in range(groups):
            value = value + jnp.where(starts[s] == tile - me, shared[s, xs], 0.0)
            value = value + jnp.where(starts[s] == tile - sibling, beside[s, xs], 0.0)
        return value

    def sourced(r):
        return chip > 0 if r == 0 else chip < line - 1

    def slot(j, c):
        xs = pl.ds(c * CHUNK, CHUNK)
        for r in range(2):
            late = chip if r == 0 else line - 1 - chip
            z = line - 1 - j + chip if r == 0 else j - line + 1 + chip

            @pl.when(late <= j)
            def _():
                part[r, z, xs] = local_sum(r, z, c)

                @pl.when(sourced(r))
                def _():
                    sum_copy(r, z, c).wait_recv()
                    part[r, z, xs] += arrived[r, z, xs]

                sum_copy(r, z, c).start()

    for step in range(chunks + line - 2):
        if step < chunks:
            c = order[step]
            others(groups, mine, lambda s: image_copy(c, s, s).wait_recv())
            beside_copy(c).start()
        for j in range(line - 2, 0, -1):
            if 0 <= step - j < chunks:
                slot(j, order[step - j])
        if step < chunks:
            c = order[step]
            beside_copy(c).wait_recv()
            slot(0, c)
    for c in order:
        for r in range(2):
            out_ref[r, pl.ds(c * CHUNK, CHUNK)] = local_sum(r, chip, c)

    for c in order:
        xs = pl.ds(c * CHUNK, CHUNK)
        for r in range(2):
            @pl.when(sourced(r))
            def _():
                sum_copy(r, chip, c).wait_recv()
                out_ref[r, xs] += arrived[r, chip, xs]

    others(groups, mine, lambda s: first_copy(s, mine).wait_send())
    for h in range(halves):
        def sent(r, z):
            src = tile_ref(h, r, z, core)
            across(h, r, z, src, core).wait_send()

            @pl.when(onward(r))
            def _():
                along(h, r, z, src).wait_send()

        each_tile(sent)
        others(groups, mine, lambda s: hand_copy(h, s, mine).wait_send())
    for c in range(chunks):
        others(groups, mine, lambda s: image_copy(c, s, mine).wait_send())
        beside_copy(c).wait_send()
        for j in range(line - 1):
            for r in range(2):
                late = chip if r == 0 else line - 1 - chip
                z = line - 1 - j + chip if r == 0 else j - line + 1 + chip

                @pl.when(late <= j)
                def _():
                    sum_copy(r, z, c).wait_send()
    for t in range(STEPS):
        drain_halo(0, t)
        drain_halo(1, t)


def body(
    courant, aperture_first, source_pos, wavelet, receiver_pos, residual, step_count,
    forward_prev, forward_now, adjoint_prev, adjoint_now,
):
    n = lax.axis_size("mp")
    groups = lax.axis_size("shot")
    tx, ny, nz = courant.shape[1:]
    recv = receiver_pos.shape[1]
    q = ny // groups
    line = n // 2
    halves = parts_of(line)
    chunks = tx // CHUNK
    smem = pl.BlockSpec(memory_space=pltpu.SMEM)
    vmem = pl.BlockSpec(memory_space=pltpu.VMEM)
    hbm = pl.BlockSpec(memory_space=pl.ANY)
    dma = pltpu.SemaphoreType.DMA
    return pl.pallas_call(
        functools.partial(kernel, n, groups, tx, ny, nz, recv),
        out_shape=jax.ShapeDtypeStruct((2, tx, q, nz), F32),
        in_specs=[smem] * 4 + [vmem] * 2 + [hbm] * 5,
        out_specs=vmem,
        scratch_shapes=[
            pltpu.VMEM((STEPS, tx + 8, ny, nz), F32),
            pltpu.VMEM((STEPS, tx + 8, ny, nz), F32),
            pltpu.VMEM((tx, ny, nz), F32),
            pltpu.VMEM((tx, ny, nz), F32),
            pltpu.VMEM((tx, ny, nz), F32),
            pltpu.VMEM((STEPS - 1, tx, ny, nz), F32),
            pltpu.VMEM((STEPS, tx, ny, nz), F32),
            pltpu.VMEM((tx, ny, nz), F32),
            pltpu.VMEM((2, n, tx, q, nz), F32),
            pltpu.VMEM((groups, tx, q, nz), F32),
            pltpu.VMEM((tx, ny, nz), F32),
            pltpu.VMEM((groups, tx, q, nz), F32),
            pltpu.VMEM((groups, tx, q, nz), F32),
            pltpu.VMEM((2, line, tx, q, nz), F32),
            pltpu.VMEM((2, line, tx, q, nz), F32),
            pltpu.VMEM((groups, 8, 128), jnp.int32),
            pltpu.VMEM((2 * nz, nz), BF16),
            pltpu.VMEM((2 * ny, 4 * ny), BF16),
            pltpu.VMEM((ny, nz), F32),
            pltpu.VMEM((3 * recv, nz), BF16),
            dma((5,)),
            dma((2, STEPS, 2)), dma((2, STEPS, 2)),
            dma((groups,)), dma((groups,)),
            dma((halves, 2, line)), dma((halves, 2, line)),
            dma((halves, 2, line)), dma((halves, 2, line)),
            dma((halves, groups)), dma((halves, groups)),
            dma((chunks, groups)), dma((chunks, groups)),
            dma((chunks,)), dma((chunks,)),
            dma((2, line, chunks)), dma((2, line, chunks)),
        ],
        compiler_params=pltpu.CompilerParams(
            collective_id=0, has_side_effects=True, vmem_limit_bytes=58 * 1024 * 1024),
    )(
        aperture_first, source_pos, wavelet, step_count,
        receiver_pos.transpose(2, 0, 1), residual,
        courant, forward_prev, forward_now, adjoint_prev, adjoint_now,
    )


def solution(mesh):
    return jax.shard_map(
        body,
        mesh=mesh,
        in_specs=(
            P(None, "mp", None, None),
            P("shot"),
            P("shot", None),
            P("shot", None),
            P("shot", None, None),
            P("shot", None, None),
            P("shot"),
            P("shot", "mp", None, None),
            P("shot", "mp", None, None),
            P("shot", "mp", None, None),
            P("shot", "mp", None, None),
        ),
        out_specs=P(None, "mp", "shot", None),
        check_vma=False,
    )
```

```python
import functools

import jax
import jax.numpy as jnp
from jax import lax
from jax.experimental import pallas as pl
from jax.experimental.pallas import tpu as pltpu
from jax.sharding import PartitionSpec as P

COEF = (-205.0 / 72.0, 1.6, -0.2, 8.0 / 315.0, -1.0 / 560.0)
F32 = jnp.float32
BF16 = jnp.bfloat16
MESH = pl.DeviceIdType.MESH
CHUNK = 4
STEPS = 4
SCALE = 5040.0
OUTER = (8064.0, -1008.0, 128.0, -9.0)


def parts_of(line):
    return 4 if line <= 4 else 2


def band(size):
    row = lax.broadcasted_iota(jnp.int32, (size, size), 0)
    col = lax.broadcasted_iota(jnp.int32, (size, size), 1)
    gap = jnp.abs(row - col)
    value = jnp.zeros((size, size), F32)
    for k in range(1, 5):
        value = jnp.where(gap == k, OUTER[k - 1], value)
    return value.astype(BF16)


def kernel(
    n, groups, tx, ny, nz, recv,
    first_ref, source_ref, wave_ref, count_ref, rec_ref, res_ref,
    courant, fprev, fnow, aprev, anow,
    out_ref,
    u_buf, w_buf, u_out, w_out, u_old, w_old, e_buf, d_buf, inj, p_buf,
    tiles, staged, img, shared, beside, part, arrived, firsts, zmat, ymat, smask, rmat,
    load_sem, halo_send, halo_recv, f_send, f_recv, a_send, a_recv, b_send, b_recv,
    x_send, x_recv, i_send, i_recv, g_send, g_recv, o_send, o_recv,
):
    me = lax.axis_index("mp")
    mine = lax.axis_index("shot")
    chip, core = lax.div(me, 2), lax.rem(me, 2)
    sibling = me + 1 - 2 * core
    line = n // 2
    q = ny // groups
    chunks = tx // CHUNK
    halves = parts_of(line)
    half = tx // halves

    def strip(s):
        return pl.ds(pl.multiple_of(s * q, q), q)

    def others(count, own, visit):
        def go(o, carry):
            visit(lax.rem(own + o, count))
            return carry

        lax.fori_loop(1, count, go, 0)

    def loop(count, visit):
        def go(o, carry):
            visit(o)
            return carry

        lax.fori_loop(0, count, go, 0)

    def remote(src, dst, send, recv_, target):
        return pltpu.make_async_remote_copy(
            src_ref=src, dst_ref=dst, send_sem=send, recv_sem=recv_,
            device_id=target, device_id_type=MESH,
        )

    barrier = pltpu.get_barrier_semaphore()
    nearby = [(me - 1, me >= 1), (me + 1, me < n - 1), (me - 2, me >= 2), (me + 2, me < n - 2)]
    for k, there in nearby:
        @pl.when(there)
        def _(k=k):
            pl.semaphore_signal(barrier, inc=1, device_id={"mp": k}, device_id_type=MESH)
    others(groups, mine, lambda s: pl.semaphore_signal(
        barrier, inc=1, device_id={"shot": s}, device_id_type=MESH))
    peers = groups - 1 + jnp.minimum(me, 2) + jnp.minimum(n - 1 - me, 2)
    pl.semaphore_wait(barrier, peers)

    def tile_ref(h, r, z, c):
        return tiles.at[r, 2 * z + c, pl.ds(h * half, half)]

    def own_ref(h, r):
        return courant.at[r, pl.ds(h * half, half), strip(mine)]

    def along(h, r, z, src):
        return remote(
            src, tile_ref(h, r, z, core), a_send.at[h, r, z], a_recv.at[h, r, z],
            {"mp": me - 2 if r == 0 else me + 2})

    def across(h, r, z, src, c):
        return remote(
            src, tile_ref(h, r, z, c), b_send.at[h, r, z], b_recv.at[h, r, z], {"mp": sibling})

    def onward(r):
        return chip > 0 if r == 0 else chip < line - 1

    def send_own(h):
        for r in range(2):
            @pl.when(onward(r))
            def _():
                along(h, r, chip, own_ref(h, r)).start()
        for r in range(2):
            across(h, r, chip, own_ref(h, r), core).start()

    def hop(h, d):
        for r in range(2):
            z = chip + d if r == 0 else chip - d
            there = z < line if r == 0 else z >= 0

            @pl.when(there)
            def _():
                along(h, r, z, tile_ref(h, r, z, core)).wait_recv()

                @pl.when(onward(r))
                def _():
                    along(h, r, z, tile_ref(h, r, z, core)).start()

                across(h, r, z, tile_ref(h, r, z, core), core).start()

    def each_tile(visit):
        for d in range(line):
            for r in range(2):
                z = chip + d if r == 0 else chip - d

                @pl.when(z < line if r == 0 else z >= 0)
                def _():
                    visit(r, z)

    def first_copy(s, sender):
        return remote(firsts.at[sender], firsts.at[sender], f_send.at[s], f_recv.at[sender], {"shot": s})

    send_own(0)
    firsts[pl.ds(mine, 1)] = jnp.full((1, 8, 128), first_ref[0], jnp.int32)
    others(groups, mine, lambda s: first_copy(s, mine).start())
    own_tile = pltpu.make_async_copy(courant.at[:, :, strip(mine)], tiles.at[:, me], load_sem.at[4])
    own_tile.start()

    def halo(f, t, side, src):
        buf = (u_buf, w_buf)[f]
        dst = buf[t].at[pl.ds(0, 4)] if side == 0 else buf[t].at[pl.ds(tx + 4, 4)]
        target = me + 1 if side == 0 else me - 1
        return remote(src, dst, halo_send.at[f, t, side], halo_recv.at[f, t, side], {"mp": target})

    def halo_src(f, t, side):
        if t == 0:
            src = (fnow, anow)[f]
            return src.at[0, pl.ds(tx - 4, 4)] if side == 0 else src.at[0, pl.ds(0, 4)]
        buf = (u_buf, w_buf)[f]
        return buf[t].at[pl.ds(tx, 4)] if side == 0 else buf[t].at[pl.ds(4, 4)]

    def send_halo(f, t):
        @pl.when(me < n - 1)
        def _():
            halo(f, t, 0, halo_src(f, t, 0)).start()

        @pl.when(me > 0)
        def _():
            halo(f, t, 1, halo_src(f, t, 1)).start()

    def wait_halo(f, t):
        @pl.when(me > 0)
        def _():
            halo(f, t, 0, halo_src(f, t, 0)).wait_recv()

        @pl.when(me < n - 1)
        def _():
            halo(f, t, 1, halo_src(f, t, 1)).wait_recv()

    def drain_halo(f, t):
        @pl.when(me < n - 1)
        def _():
            halo(f, t, 0, halo_src(f, t, 0)).wait_send()

        @pl.when(me > 0)
        def _():
            halo(f, t, 1, halo_src(f, t, 1)).wait_send()

    loads = [
        pltpu.make_async_copy(fnow.at[0], u_buf[0].at[pl.ds(4, tx)], load_sem.at[0]),
        pltpu.make_async_copy(anow.at[0], w_buf[0].at[pl.ds(4, tx)], load_sem.at[1]),
        pltpu.make_async_copy(fprev.at[0], u_old, load_sem.at[2]),
        pltpu.make_async_copy(aprev.at[0], w_old, load_sem.at[3]),
    ]
    for copy in loads:
        copy.start()

    edge = jnp.zeros((4, ny, nz), F32)

    @pl.when(me == 0)
    def _():
        for t in range(STEPS):
            u_buf[t][pl.ds(0, 4)] = edge
            w_buf[t][pl.ds(0, 4)] = edge

    @pl.when(me == n - 1)
    def _():
        for t in range(STEPS):
            u_buf[t][pl.ds(tx + 4, 4)] = edge
            w_buf[t][pl.ds(tx + 4, 4)] = edge

    band_z, band_y = band(nz), band(ny)
    zmat[pl.ds(0, nz)] = band_z
    zmat[pl.ds(nz, nz)] = band_z
    blank = jnp.zeros((ny, 2 * ny), BF16)
    pair = jnp.concatenate([band_y, band_y], axis=1)
    ymat[pl.ds(0, ny)] = jnp.concatenate([pair, blank], axis=1)
    ymat[pl.ds(ny, ny)] = jnp.concatenate([blank, pair], axis=1)
    y_id = lax.broadcasted_iota(jnp.int32, (ny, nz), 0)
    z_id = lax.broadcasted_iota(jnp.int32, (ny, nz), 1)
    smask[...] = jnp.where((y_id == source_ref[0, 1]) & (z_id == source_ref[0, 2]), 1.0, 0.0)
    same = (lax.broadcasted_iota(jnp.int32, (recv, recv), 0)
            == lax.broadcasted_iota(jnp.int32, (recv, recv), 1))
    at_z = jnp.sum(jnp.where(same, rec_ref[2].astype(F32), 0.0), axis=1, keepdims=True)
    hit_z = at_z.astype(jnp.int32) == lax.broadcasted_iota(jnp.int32, (recv, nz), 1)
    hit_z = jnp.where(hit_z, 1.0, 0.0).astype(BF16)
    for i in range(3):
        rmat[pl.ds(i * recv, recv)] = hit_z
    res = res_ref[0]
    res0 = res.astype(BF16).astype(F32)
    res1 = (res - res0).astype(BF16).astype(F32)
    res2 = res - res0 - res1
    res_all = jnp.concatenate([res0, res1, res2], axis=1)
    rec_x = jnp.concatenate([rec_ref[0]] * 3, axis=1)
    rec_y = jnp.concatenate([rec_ref[1]] * 3, axis=1)
    hit_y = lax.broadcasted_iota(jnp.int32, (ny, 3 * recv), 0) == rec_y
    hit_y = jnp.where(hit_y, 1.0, 0.0)

    def inject(c):
        x0 = c * CHUNK
        for s in range(STEPS):
            rows = []
            for i in range(CHUNK):
                at_x = jnp.where(rec_x == me * tx + x0 + i, res_all[s:s + 1], 0.0)
                rows.append((hit_y * at_x).astype(BF16))
            field = jnp.dot(jnp.concatenate(rows, axis=0), rmat[...], preferred_element_type=F32)
            inj[s, pl.ds(x0, CHUNK)] = field.reshape(CHUNK, ny, nz)

    def hand_copy(h, s, sender):
        xs = pl.ds(h * half, half)
        return remote(
            staged.at[s, xs], p_buf.at[xs, strip(sender)],
            x_send.at[h, s], x_recv.at[h, sender], {"shot": s})

    def picked(s, x):
        first = jnp.max(firsts[pl.ds(s, 1)])
        value = jnp.zeros((1, q, nz), F32)
        for k in range(n + 1):
            t = me + k
            value = jnp.where(first == k, tiles[lax.div(t, n), lax.rem(t, n), pl.ds(x, 1)], value)
        return value

    def hand(h):
        each_tile(lambda r, z: across(h, r, z, tile_ref(h, r, z, core), 1 - core).wait_recv())

        def give(s):
            def plane(i):
                staged[pl.ds(s, 1), pl.ds(h * half + i, 1)] = picked(s, h * half + i)[None]

            loop(half, plane)
            hand_copy(h, s, mine).start()

        others(groups, mine, give)

        def keep(i):
            p_buf[pl.ds(h * half + i, 1), strip(mine)] = picked(mine, h * half + i)

        loop(half, keep)

    for h in range(1, min(2, halves)):
        send_own(h)
    levels = halves + line - 2
    for level in range(1, levels + 1):
        for h in range(halves):
            if 1 <= level - h < line:
                hop(h, level - h)
        if level + 1 < halves:
            send_own(level + 1)
        if level == levels - 1:
            send_halo(0, 0)
            send_halo(1, 0)
        if level <= chunks:
            inject(level - 1)
        h = level - line + 1
        if h == 0:
            own_tile.wait()
            others(groups, mine, lambda s: first_copy(s, s).wait_recv())
        if h >= 0:
            hand(h)

    rows = 32

    def across_plane(buf, out, t, x0):
        centre = buf[t][pl.ds(x0 + 4, CHUNK)].reshape(CHUNK * ny, nz)
        high = centre.astype(BF16)
        low = (centre - high.astype(F32)).astype(BF16)
        out[...] = jnp.dot(
            jnp.concatenate([high, low], axis=1), zmat[...], preferred_element_type=F32)
        for i in range(0, CHUNK, 2):
            one, two = slice(i * ny, (i + 1) * ny), slice((i + 1) * ny, (i + 2) * ny)
            stack = jnp.concatenate([high[one], low[one], high[two], low[two]], axis=0)
            out[pl.ds(i * ny, 2 * ny)] += jnp.dot(ymat[...], stack, preferred_element_type=F32)

    def each_block(x0, visit):
        for i in range(CHUNK):
            for y0 in range(0, ny, rows):
                visit(x0 + i, pl.ds(y0, rows), pl.ds(i * ny + y0, rows))

    def lap(buf, out, t, x, ys, flat):
        field = buf[t]
        total = out[flat] * (1.0 / SCALE) + 3.0 * COEF[0] * field[x + 4, ys]
        for k in range(1, 5):
            total = total + COEF[k] * (field[x + 4 + k, ys] + field[x + 4 - k, ys])
        return total

    count = count_ref[0]
    source_x = source_ref[0, 0] - me * tx

    def drive(t, x, ys, flat):
        amount = jnp.where(source_x == x, wave_ref[0, t], 0.0)
        total = lap(u_buf, u_out, t, x, ys, flat) + smask[ys] * amount
        if t >= 2:
            total = jnp.where(t < count, total, 0.0)
        return total

    def forward(t, x0):
        if t:
            across_plane(u_buf, u_out, t, x0)

        def block(x, ys, flat):
            if t == 0:
                total, before = d_buf[0][x, ys], u_old[x, ys]
            else:
                total = drive(t, x, ys, flat)
                d_buf[t][x, ys] = total
                before = u_buf[t - 1][x + 4, ys]
            u_buf[t + 1][x + 4, ys] = 2.0 * u_buf[t][x + 4, ys] - before + p_buf[x, ys] * total

        each_block(x0, block)

    def backward(t, x, ys, flat):
        s = STEPS - 1 - t
        total = e_buf[x, ys] if t == 0 else lap(w_buf, w_out, t, x, ys, flat) + inj[s, x, ys]
        now = w_buf[t][x + 4, ys]
        before = w_buf[t - 1][x + 4, ys] if s + 1 < 2 else w_old[x, ys]
        new = 2.0 * now - before + p_buf[x, ys] * total
        if s >= 2:
            w_old[x, ys] = jnp.where(s < count, now, before)
            new = jnp.where(s < count, new, now)
        return new

    def adjoint(t, x0):
        if t:
            across_plane(w_buf, w_out, t, x0)

        def block(x, ys, flat):
            w_buf[t + 1][x + 4, ys] = backward(t, x, ys, flat)

        each_block(x0, block)

    last = tx - CHUNK
    faces = lambda visit: loop(2, lambda i: visit(i * last))
    inner = lambda visit: loop(chunks - 2, lambda i: visit(CHUNK + i * CHUNK))

    for copy in loads:
        copy.wait()

    def early(x0):
        across_plane(u_buf, u_out, 0, x0)
        across_plane(w_buf, w_out, 0, x0)

        def block(x, ys, flat):
            d_buf[0][x, ys] = drive(0, x, ys, flat)
            e_buf[x, ys] = lap(w_buf, w_out, 0, x, ys, flat) + inj[STEPS - 1, x, ys]

        each_block(x0, block)

    inner(early)
    wait_halo(0, 0)
    wait_halo(1, 0)
    faces(early)

    for h in range(halves):
        others(groups, mine, lambda s: hand_copy(h, s, s).wait_recv())

    for t in range(STEPS - 1):
        if t:
            wait_halo(0, t)
        faces(functools.partial(forward, t))
        send_halo(0, t + 1)
        inner(functools.partial(forward, t))
        if t:
            wait_halo(1, t)
        faces(functools.partial(adjoint, t))
        send_halo(1, t + 1)
        inner(functools.partial(adjoint, t))

    def image_copy(c, s, sender):
        xs = pl.ds(c * CHUNK, CHUNK)
        return remote(
            img.at[xs, strip(s)], shared.at[sender, xs],
            i_send.at[c, s], i_recv.at[c, sender], {"shot": s})

    def final(x0):
        own = pl.ds(x0, CHUNK)
        t = STEPS - 1
        across_plane(u_buf, u_out, t, x0)
        across_plane(w_buf, w_out, t, x0)

        def block(x, ys, flat):
            new = backward(t, x, ys, flat) * d_buf[0][x, ys]
            new = new + w_buf[1][x + 4, ys] * drive(t, x, ys, flat)
            for k in range(1, t):
                new = new + w_buf[k + 1][x + 4, ys] * d_buf[t - k][x, ys]
            img[x, ys] = new

        each_block(x0, block)
        c = lax.div(x0, CHUNK)
        others(groups, mine, lambda s: image_copy(c, s, mine).start())
        shared[pl.ds(mine, 1), own] = img[own, strip(mine)].reshape(1, CHUNK, q, nz)

    inner(final)
    wait_halo(0, STEPS - 1)
    wait_halo(1, STEPS - 1)
    faces(final)

    def beside_copy(c):
        xs = pl.ds(c * CHUNK, CHUNK)
        return remote(shared.at[:, xs], beside.at[:, xs], g_send.at[c], g_recv.at[c], {"mp": sibling})

    order = list(range(1, chunks - 1)) + [0, chunks - 1]
    starts = [jnp.max(firsts[s]) for s in range(groups)]

    def sum_copy(r, z, c):
        xs = pl.ds(c * CHUNK, CHUNK)
        return remote(
            part.at[r, z, xs], arrived.at[r, z, xs], o_send.at[r, z, c], o_recv.at[r, z, c],
            {"mp": me + 2 if r == 0 else me - 2})

    def local_sum(r, z, c):
        tile = r * n + 2 * z + core
        xs = pl.ds(c * CHUNK, CHUNK)
        value = jnp.zeros((CHUNK, q, nz), F32)
        for s in range(groups):
            value = value + jnp.where(starts[s] == tile - me, shared[s, xs], 0.0)
            value = value + jnp.where(starts[s] == tile - sibling, beside[s, xs], 0.0)
        return value

    def sourced(r):
        return chip > 0 if r == 0 else chip < line - 1

    def slot(j, c):
        xs = pl.ds(c * CHUNK, CHUNK)
        for r in range(2):
            late = chip if r == 0 else line - 1 - chip
            z = line - 1 - j + chip if r == 0 else j - line + 1 + chip

            @pl.when(late <= j)
            def _():
                part[r, z, xs] = local_sum(r, z, c)

                @pl.when(sourced(r))
                def _():
                    sum_copy(r, z, c).wait_recv()
                    part[r, z, xs] += arrived[r, z, xs]

                sum_copy(r, z, c).start()

    for step in range(chunks + line - 2):
        if step < chunks:
            c = order[step]
            others(groups, mine, lambda s: image_copy(c, s, s).wait_recv())
            beside_copy(c).start()
        for j in range(line - 2, 0, -1):
            if 0 <= step - j < chunks:
                slot(j, order[step - j])
        if step < chunks:
            c = order[step]
            beside_copy(c).wait_recv()
            slot(0, c)
    for c in order:
        for r in range(2):
            out_ref[r, pl.ds(c * CHUNK, CHUNK)] = local_sum(r, chip, c)

    for c in order:
        xs = pl.ds(c * CHUNK, CHUNK)
        for r in range(2):
            @pl.when(sourced(r))
            def _():
                sum_copy(r, chip, c).wait_recv()
                out_ref[r, xs] += arrived[r, chip, xs]

    others(groups, mine, lambda s: first_copy(s, mine).wait_send())
    for h in range(halves):
        def sent(r, z):
            src = tile_ref(h, r, z, core)
            across(h, r, z, src, core).wait_send()

            @pl.when(onward(r))
            def _():
                along(h, r, z, src).wait_send()

        each_tile(sent)
        others(groups, mine, lambda s: hand_copy(h, s, mine).wait_send())
    for c in range(chunks):
        others(groups, mine, lambda s: image_copy(c, s, mine).wait_send())
        beside_copy(c).wait_send()
        for j in range(line - 1):
            for r in range(2):
                late = chip if r == 0 else line - 1 - chip
                z = line - 1 - j + chip if r == 0 else j - line + 1 + chip

                @pl.when(late <= j)
                def _():
                    sum_copy(r, z, c).wait_send()
    for t in range(STEPS):
        drain_halo(0, t)
        drain_halo(1, t)


def body(
    courant, aperture_first, source_pos, wavelet, receiver_pos, residual, step_count,
    forward_prev, forward_now, adjoint_prev, adjoint_now,
):
    n = lax.axis_size("mp")
    groups = lax.axis_size("shot")
    tx, ny, nz = courant.shape[1:]
    recv = receiver_pos.shape[1]
    q = ny // groups
    line = n // 2
    halves = parts_of(line)
    chunks = tx // CHUNK
    smem = pl.BlockSpec(memory_space=pltpu.SMEM)
    vmem = pl.BlockSpec(memory_space=pltpu.VMEM)
    hbm = pl.BlockSpec(memory_space=pl.ANY)
    dma = pltpu.SemaphoreType.DMA
    return pl.pallas_call(
        functools.partial(kernel, n, groups, tx, ny, nz, recv),
        out_shape=jax.ShapeDtypeStruct((2, tx, q, nz), F32),
        in_specs=[smem] * 4 + [vmem] * 2 + [hbm] * 5,
        out_specs=vmem,
        scratch_shapes=[
            [pltpu.VMEM((tx + 8, ny, nz), F32)] * STEPS,
            [pltpu.VMEM((tx + 8, ny, nz), F32)] * STEPS,
            pltpu.VMEM((CHUNK * ny, nz), F32),
            pltpu.VMEM((CHUNK * ny, nz), F32),
            pltpu.VMEM((tx, ny, nz), F32),
            pltpu.VMEM((tx, ny, nz), F32),
            pltpu.VMEM((tx, ny, nz), F32),
            [pltpu.VMEM((tx, ny, nz), F32)] * (STEPS - 1),
            pltpu.VMEM((STEPS, tx, ny, nz), F32),
            pltpu.VMEM((tx, ny, nz), F32),
            pltpu.VMEM((2, n, tx, q, nz), F32),
            pltpu.VMEM((groups, tx, q, nz), F32),
            pltpu.VMEM((tx, ny, nz), F32),
            pltpu.VMEM((groups, tx, q, nz), F32),
            pltpu.VMEM((groups, tx, q, nz), F32),
            pltpu.VMEM((2, line, tx, q, nz), F32),
            pltpu.VMEM((2, line, tx, q, nz), F32),
            pltpu.VMEM((groups, 8, 128), jnp.int32),
            pltpu.VMEM((2 * nz, nz), BF16),
            pltpu.VMEM((2 * ny, 4 * ny), BF16),
            pltpu.VMEM((ny, nz), F32),
            pltpu.VMEM((3 * recv, nz), BF16),
            dma((5,)),
            dma((2, STEPS, 2)), dma((2, STEPS, 2)),
            dma((groups,)), dma((groups,)),
            dma((halves, 2, line)), dma((halves, 2, line)),
            dma((halves, 2, line)), dma((halves, 2, line)),
            dma((halves, groups)), dma((halves, groups)),
            dma((chunks, groups)), dma((chunks, groups)),
            dma((chunks,)), dma((chunks,)),
            dma((2, line, chunks)), dma((2, line, chunks)),
        ],
        compiler_params=pltpu.CompilerParams(
            collective_id=0, has_side_effects=True, vmem_limit_bytes=58 * 1024 * 1024),
    )(
        aperture_first, source_pos, wavelet, step_count,
        receiver_pos.transpose(2, 0, 1), residual,
        courant, forward_prev, forward_now, adjoint_prev, adjoint_now,
    )


def solution(mesh):
    return jax.shard_map(
        body,
        mesh=mesh,
        in_specs=(
            P(None, "mp", None, None),
            P("shot"),
            P("shot", None),
            P("shot", None),
            P("shot", None, None),
            P("shot", None, None),
            P("shot"),
            P("shot", "mp", None, None),
            P("shot", "mp", None, None),
            P("shot", "mp", None, None),
            P("shot", "mp", None, None),
        ),
        out_specs=P(None, "mp", "shot", None),
        check_vma=False,
    )
```
